128 devices in a mesh: blk: 32 (over z, y, core), pair: 4 (over x).
Axes of the slice: x: 4, y: 4, z: 4, core: 2. Of those that a mesh axis runs over, the one named last changes fastest.
Arguments:
- basis: float32 [8, 256, 510, 128], P(None, ('blk', 'pair'))
- mie_coeffs: float32 [256, 510, 128], P(('blk', 'pair')), may hold values from -8 to 8
- rot_table: bfloat16 [8, 510, 510], replicated, may hold values from -0.25 to 0.25
- axial_table: bfloat16 [8, 2, 510, 510], replicated, may hold values from -0.1875 to 0.1875
- pair_table: int32 [32, 128, 3], P('blk'), may hold values from 0 to 23, as said below
- pair_count: int32 [32], P('blk'), may hold values from 32 to 128, as said below
Outputs:
- projections: float32 [2, 8], replicated
- next_basis: float32 [256, 510, 128], P(('blk', 'pair'))
The draws below stay inside these ranges and needn't reach their ends.
Inputs may be any that keep to these rules, and one draw needn't show every extreme that they name: `pair_table`: row p of blk index i is (a, b, g): a names one of the 8 blocks of blk index i; b counts from the first block of blk index i - 1 and is never a + 8; on blk index 0, b >= 8; on the last, b < 16; g < 8. Rows from pair_count on are ignored. `pair_count`: some blk index lists all 128 rows.
All inputs are finite; a program needn't handle non-finite values.
Results may differ from the reference program's by a relative error of at most 0.0003.
Values may be sent and summed in bfloat16 or wider, within the bound.
A program may use at most 128 MiB of HBM per device.

```python
import jax
import jax.numpy as jnp
from jax import lax

MODES = 510
SPHERES = 64
BLK_DEV = 8
PAIR_MAX = 128
TABLES = 8
KRYLOV = 8
BLOCKS = 256
N_BLK = 32


def draw_basis(key, part):
    key = jax.random.fold_in(key, 11)
    keys = jax.random.split(key, 4)
    shape = (KRYLOV, BLOCKS, MODES, 2 * SPHERES)
    rise = jnp.exp(jnp.log(3.0) * jnp.arange(BLOCKS, dtype=jnp.float32) / (BLOCKS - 1))
    rise = rise[None, :, None, None]
    row_scale = jnp.exp(jnp.log(10.0) * jax.random.uniform(keys[0], (1, BLOCKS, MODES, 1), jnp.float32))
    column_scale = jnp.exp(jnp.log(10.0) * jax.random.uniform(keys[1], (1, 1, 1, 2 * SPHERES), jnp.float32))
    common = jax.random.normal(keys[2], (1, BLOCKS, MODES, 2 * SPHERES), jnp.float32)
    own = jax.random.normal(keys[3], shape, jnp.float32)
    shared_weight = 0.5
    return (0.7 * own + shared_weight * common) * rise * row_scale * column_scale


def draw_pair_count(key, part):
    key = jax.random.fold_in(key, 23)
    keys = jax.random.split(key, 2)
    uneven = jax.random.randint(keys[0], (N_BLK,), 0, 1001)
    counts = PAIR_MAX // 4 + 3 * PAIR_MAX // 4 * uneven * uneven // 1000000
    busiest = jax.random.randint(keys[1], (), 0, N_BLK)
    return jnp.where(jnp.arange(N_BLK) == busiest, PAIR_MAX, counts).astype(jnp.int32)


def draw_pair_table(key, part):
    key = jax.random.fold_in(key, 37)
    keys = jax.random.split(key, 3)
    target = jax.random.randint(keys[0], (N_BLK, PAIR_MAX), 0, BLK_DEV)
    device_row = jnp.arange(N_BLK)[:, None]
    lowest = jnp.where(device_row > 0, 0, BLK_DEV)
    highest = jnp.where(device_row < N_BLK - 1, 3 * BLK_DEV, 2 * BLK_DEV)
    raw_source = jax.random.randint(keys[1], (N_BLK, PAIR_MAX), 0, 1 << 20)
    source = lowest + raw_source % (highest - lowest)
    source = jnp.where(source == target + BLK_DEV, lowest + (source - lowest + 1) % (highest - lowest), source)
    source = source.at[0, PAIR_MAX - 1].set(3 * BLK_DEV - 1)
    entry = jax.random.randint(keys[2], (N_BLK, PAIR_MAX), 0, TABLES)
    return jnp.stack([target, source, entry], axis=-1).astype(jnp.int32)


def block_scale(stream_key, shape, cuts, least, high):
    gain, own = 1.0, jax.random.fold_in(stream_key, 6)
    for dim, shards_of in cuts:
        draws = jnp.exp(jax.random.uniform(jax.random.fold_in(own, dim), (shards_of,), jnp.float32, least / len(cuts), high / len(cuts)))
        gain = gain * jnp.repeat(draws, shape[dim] // shards_of).reshape([-1 if axis == dim else 1 for axis in range(len(shape))])
    return gain


def centred(stream_key, extent, scale, limit, pieces=(), kind=jnp.bfloat16):
    result = scale * jax.random.normal(stream_key, extent, jnp.float32)
    if pieces:
        result = result * block_scale(stream_key, extent, pieces, -0.22, 0.18)
    return jnp.clip(result, -limit, limit).astype(kind)


def setup_inputs(seed: int = 0) -> dict:
    seeds = jax.random.split(jax.random.key(seed), 7)
    basis = draw_basis(jax.random.fold_in(seeds[6], 71), 0)
    mie_coeffs = centred(seeds[1], (BLOCKS, MODES, 2 * SPHERES), 2.0, 8.0, ((0, 128),), jnp.float32)
    rot_table = centred(seeds[2], (TABLES, MODES, MODES), MODES ** -0.5, 0.25)
    axial_table = centred(seeds[3], (TABLES, 2, MODES, MODES), (2 * MODES) ** -0.5, 0.1875)
    pair_table = draw_pair_table(jax.random.fold_in(seeds[6], 71), 0)
    pair_count = draw_pair_count(jax.random.fold_in(seeds[6], 71), 0)
    return {"basis": basis, "mie_coeffs": mie_coeffs, "rot_table": rot_table, "axial_table": axial_table, "pair_table": pair_table, "pair_count": pair_count}


batch_pairs = 8

def swap_parts(packed):
    half_width = packed.shape[-1] // 2
    return jnp.concatenate([-packed[..., half_width:], packed[..., :half_width]], axis=-1)

def complex_product(left, right):
    half_width = left.shape[-1] // 2
    left_real, left_imag = (left[..., :half_width], left[..., half_width:])
    right_real, right_imag = (right[..., :half_width], right[..., half_width:])
    return jnp.concatenate([left_real * right_real - left_imag * right_imag, left_real * right_imag + left_imag * right_real], axis=-1)

def translate(rotation, axial_pair, source, transposed):
    turned = jnp.einsum('pij,pjk->pik', rotation, source)
    turned = lax.optimization_barrier(turned.astype(jnp.bfloat16)).astype(jnp.float32)
    stacked = jnp.stack([turned, swap_parts(turned)], axis=1)
    if transposed:
        moved = jnp.einsum('pcji,pcjk->pik', axial_pair, stacked)
    else:
        moved = jnp.einsum('pcij,pcjk->pik', axial_pair, stacked)
    moved = lax.optimization_barrier(moved.astype(jnp.bfloat16)).astype(jnp.float32)
    return jnp.einsum('pji,pjk->pik', rotation, moved)

def reference(basis, mie_coeffs, rot_table, axial_table, pair_table, pair_count):
    coeff = basis[KRYLOV - 1].astype(jnp.bfloat16)
    flat_rows = pair_table.reshape(-1, 3)
    position = jnp.arange(N_BLK * PAIR_MAX, dtype=jnp.int32)
    owner = position // PAIR_MAX
    live = position % PAIR_MAX < pair_count[owner]
    target = owner * BLK_DEV + flat_rows[:, 0]
    source = jnp.clip((owner - 1) * BLK_DEV + flat_rows[:, 1], 0, BLOCKS - 1)
    groups = (target.reshape(-1, batch_pairs), source.reshape(-1, batch_pairs), flat_rows[:, 2].reshape(-1, batch_pairs), live.reshape(-1, batch_pairs))

    def accumulate(scattered, group):
        target_rows, source_rows, table_rows, live_rows = group
        rotation = rot_table[table_rows].astype(jnp.float32)
        axial_pair = axial_table[table_rows].astype(jnp.float32)
        forward = translate(rotation, axial_pair, coeff[source_rows].astype(jnp.float32), False)
        backward = translate(rotation, axial_pair, coeff[target_rows].astype(jnp.float32), True)
        forward = jnp.where(live_rows[:, None, None], forward, jnp.float32(0.0))
        backward = jnp.where(live_rows[:, None, None], backward, jnp.float32(0.0))
        scattered = scattered.at[target_rows].add(forward).at[source_rows].add(backward)
        return (scattered, None)
    start_field = jnp.zeros((BLOCKS, MODES, 2 * SPHERES), jnp.float32)
    scattered, unused = lax.scan(accumulate, start_field, groups)
    image = basis[KRYLOV - 1] - complex_product(mie_coeffs, scattered)
    mean_scale = 1.0 / (BLOCKS * MODES * 2 * SPHERES)
    highest = lax.Precision.HIGHEST
    real_part = jnp.einsum('kbcs,bcs->k', basis, image, precision=highest) * mean_scale
    imag_part = -jnp.einsum('kbcs,bcs->k', basis, swap_parts(image), precision=highest) * mean_scale
    remainder = image - jnp.einsum('k,kbcs->bcs', real_part, basis, precision=highest)
    remainder = remainder - jnp.einsum('k,kbcs->bcs', imag_part, swap_parts(basis), precision=highest)
    norm_square = jnp.sum(remainder * remainder) * mean_scale
    next_basis = remainder * lax.rsqrt(norm_square)
    return (jnp.stack([real_part, imag_part]), next_basis)
```

```python
import functools

import jax
import jax.numpy as jnp
from jax import lax
from jax.experimental import pallas as pl
from jax.experimental.pallas import tpu as pltpu
from jax.sharding import PartitionSpec as P

MESH = pl.DeviceIdType.MESH
F32 = jnp.float32
BF16 = jnp.bfloat16
MODES = 510
PAD = 512
KRYLOV = 8
TABLES = 8
BLOCKS = 256
SPHERES = 64
ROWS = 16
CHUNKS = 4
MEAN_SCALE = 1.0 / (BLOCKS * MODES * 2 * SPHERES)

NT = (((1,), (1,)), ((), ()))
NN = (((1,), (0,)), ((), ()))


def dot(left, right, dims):
    return lax.dot_general(left, right, dims, preferred_element_type=F32)


def times_i(value):
    lane = lax.broadcasted_iota(jnp.int32, value.shape, 1)
    turned = pltpu.roll(value, SPHERES, axis=1)
    return jnp.where(lane < SPHERES, -turned, turned)


def fold(value):
    rows = value.shape[0]
    whole = rows // 8 * 8
    total = value[:8]
    for start in range(8, whole, 8):
        total = total + value[start : start + 8]
    if rows > whole:
        rest = value[whole:]
        total = total + jnp.concatenate([rest, jnp.zeros((8 - rest.shape[0], 128), F32)], axis=0)
    return total


def row_pieces(step):
    return [(start, min(step, MODES - start)) for start in range(0, MODES, step)]


def pair_rows(table, count):
    across = jnp.transpose(table)[:8]
    lane = lax.broadcasted_iota(jnp.int32, (8, 128), 1)
    row = lax.broadcasted_iota(jnp.int32, (8, 128), 0)
    return jnp.where((row == 2) & (lane >= count), -1.0, across)


def count_matrix(pairs, member):
    row = lax.broadcasted_iota(jnp.int32, (256, 128), 0)
    g_row = (row >> 5).astype(F32)
    back = ((row >> 4) & 1) == 1
    own = (2 * member + ((row >> 3) & 1)).astype(F32)
    column = (lax.broadcasted_iota(jnp.int32, (192, 128), 0) >> 3).astype(F32)
    total = None
    for off, back_here in ((1, False), (0, True), (1, True), (2, True)):
        a, b, g = (pairs[off][n : n + 1] for n in range(3))
        right_table = jnp.where(g_row == g, 1.0, 0.0)
        if back_here:
            hit = jnp.where(back & (own + 8.0 * (2 - off) == b), right_table, 0.0)
            place = jnp.where(column == a + 8.0 * off, 1.0, 0.0)
        else:
            hit = jnp.where((~back) & (own == a), right_table, 0.0)
            place = jnp.where(column == b, 1.0, 0.0)
        term = dot(hit.astype(BF16), place.astype(BF16), NT)
        total = term if total is None else total + term
    same = (lax.broadcasted_iota(jnp.int32, (256, 192), 0) & 7) == (
        lax.broadcasted_iota(jnp.int32, (256, 192), 1) & 7
    )
    return jnp.where(same, total, 0.0).astype(BF16)


def aggregate(counts, win, sums, group):
    halves = []
    for slab in (2 * group, 2 * group + 1):
        part = win[:, slab].reshape(12 * ROWS, PAD)
        halves.append(dot(counts, part, NN).reshape(32, 8, PAD))
    sums[group] = jnp.concatenate(halves, axis=1).astype(BF16)[:, :, :MODES]


def chain(g, groups, sums, rot, axial):
    half = len(groups) // 2
    parts = []
    for direction in range(2):
        for imag in range(2):
            for t in range(2):
                for n in groups[imag * half : imag * half + half]:
                    parts.append(sums[n, g * 4 + direction * 2 + t])
    rotation = rot[g]
    first, second = axial[g, 0], axial[g, 1]
    turned = dot(jnp.concatenate(parts, axis=0), rotation, NT).astype(BF16)
    count = turned.shape[0] // 2
    forward, backward = turned[:count], turned[count:]

    def swapped(value):
        return jnp.concatenate([-value[count // 2 :], value[: count // 2]], axis=0)

    moved = dot(forward, first, NT) + dot(swapped(forward), second, NT)
    moved = moved + dot(backward, first, NN) + dot(swapped(backward), second, NN)
    return dot(moved.astype(BF16), rotation, NN)


def field_of(groups, half, sums, rot, axial, field, acc):
    def step(g, carry):
        value = chain(g, groups, sums, rot, axial)
        acc[...] = jnp.where(g == 0, value, acc[...] + value)
        return carry

    lax.fori_loop(0, TABLES, step, 0)
    width = 8 * len(groups)
    for imag in range(2):
        for t in range(2):
            start = (imag * 2 + t) * width
            field[t, pl.ds(imag * 64 + half * 32, width), pl.ds(0, MODES)] = acc[pl.ds(start, width), :]


def kernel(
    basis_hbm, mie_hbm, rot_hbm, axial_hbm, table_hbm, count_ref,
    proj_ref, out_ref,
    basis, mie, rot, axial, table, wide, current, pairs, win, sums, acc, field, image, red_a, red_b,
    load_sem, send_sem, recv_sem, pair_send, pair_recv, a_send, a_recv, b_send, b_recv,
):
    blk_ways, pair_ways = lax.axis_size("blk"), lax.axis_size("pair")
    blk, member = lax.axis_index("blk"), lax.axis_index("pair")
    core = lax.rem(blk, 2)
    row = blk // 2
    row_ways = blk_ways // 2
    inner = blk + 1 - 2 * core
    outer = lax.rem(blk - 1 + 2 * core + blk_ways, blk_ways)
    right, left, far = (lax.rem(member + n, pair_ways) for n in (1, 3, 2))

    last = KRYLOV - 1
    loads = [
        pltpu.make_async_copy(basis_hbm.at[last], basis.at[last], load_sem.at[0]),
        pltpu.make_async_copy(table_hbm.at[0], table, load_sem.at[1]),
        pltpu.make_async_copy(basis_hbm.at[pl.ds(0, last)], basis.at[pl.ds(0, last)], load_sem.at[2]),
        pltpu.make_async_copy(mie_hbm, mie, load_sem.at[3]),
        pltpu.make_async_copy(rot_hbm, rot, load_sem.at[4]),
        pltpu.make_async_copy(axial_hbm, axial, load_sem.at[5]),
    ]
    for load in loads:
        load.start()

    spot = core * pair_ways + member
    group_a = []
    for n in range(1, 2 * pair_ways):
        other = lax.rem(spot + n, 2 * pair_ways)
        group_a.append((other, (2 * row + other // pair_ways, lax.rem(other, pair_ways))))
    group_b = []
    for n in range(1, row_ways):
        other = lax.rem(row + n, row_ways)
        group_b.append((other, (2 * other + core, member)))
    barrier = pltpu.get_barrier_semaphore()
    for device in [(outer, member)] + [d for _, d in group_a] + [d for _, d in group_b]:
        pl.semaphore_signal(barrier, inc=1, device_id=device, device_id_type=MESH)

    loads[0].wait()
    current[:, pl.ds(MODES - 6, 8), :] = jnp.zeros((2, 8, 128), F32)
    mine = 4 + member
    for t in range(2):
        current[t, pl.ds(0, MODES), :] = basis[last, t]
    flipped = [jnp.transpose(current[t]) for t in range(2)]
    for slab in range(16):
        half, imag, q = slab // 8, slab // 4 % 2, slab % 4
        start = imag * 64 + half * 32 + q * 8
        both = jnp.concatenate([value[start : start + 8] for value in flipped], axis=0)
        win[mine, slab] = both.astype(BF16)
    pl.semaphore_wait(barrier, 1 + len(group_a) + len(group_b))

    width = 16 // CHUNKS
    sends = []

    def send(source_slot, target_slot, chunk, device):
        place = pl.ds(chunk * width, width)
        copy = pltpu.make_async_remote_copy(
            src_ref=win.at[source_slot, place],
            dst_ref=win.at[target_slot, place],
            send_sem=send_sem.at[len(sends)],
            recv_sem=recv_sem.at[target_slot * CHUNKS + chunk],
            device_id=device,
            device_id_type=MESH,
        )
        copy.start()
        sends.append(copy)

    def arrived(slot, chunk):
        place = pl.ds(chunk * width, width)
        pltpu.make_async_remote_copy(
            src_ref=win.at[slot, place],
            dst_ref=win.at[slot, place],
            send_sem=send_sem.at[0],
            recv_sem=recv_sem.at[slot * CHUNKS + chunk],
            device_id=(inner, member),
            device_id_type=MESH,
        ).wait_recv()

    to_inner, to_outer = 8 * core, 8 * (1 - core)
    from_inner, from_outer = 8 * (1 - core), 8 * core
    for chunk in range(CHUNKS):
        send(mine, to_outer + member, chunk, (outer, member))
        send(mine, mine, chunk, (blk, right))
        send(mine, mine, chunk, (blk, left))
        send(mine, to_inner + member, chunk, (inner, member))

    loads[1].wait()
    wide[...] = jnp.zeros((128, 128), F32)
    wide[:, pl.ds(0, 3)] = table[...].astype(F32)
    pairs[1] = pair_rows(wide[...], count_ref[0])
    pair_copies = []
    for n, (slot, device) in enumerate(((2 * core, (inner, member)), (2 - 2 * core, (outer, member)))):
        copy = pltpu.make_async_remote_copy(
            src_ref=pairs.at[1],
            dst_ref=pairs.at[slot],
            send_sem=pair_send.at[n],
            recv_sem=pair_recv.at[n],
            device_id=device,
            device_id_type=MESH,
        )
        copy.start()
        pair_copies.append(copy)

    def forward(chunk):
        for origin, keep_on, device in ((left, 0, right), (right, 1, left)):
            arrived(4 + origin, chunk)
            send(4 + origin, to_outer + origin, chunk, (outer, member))
            if chunk % 2 == keep_on:
                send(4 + origin, 4 + origin, chunk, (blk, device))
            send(4 + origin, to_inner + origin, chunk, (inner, member))

    def forward_far(chunk):
        arrived(4 + far, chunk)
        send(4 + far, to_outer + far, chunk, (outer, member))
        send(4 + far, to_inner + far, chunk, (inner, member))

    def landed(chunks):
        for chunk in chunks:
            for n in range(pair_ways):
                arrived(from_inner + n, chunk)
                arrived(from_outer + n, chunk)

    forward(0)
    forward(1)
    forward_far(0)
    forward(2)
    forward_far(1)
    forward(3)
    forward_far(2)
    forward_far(3)
    for copy in pair_copies:
        copy.wait()
    counts = count_matrix([pairs[n] for n in range(3)], member)
    loads[4].wait()
    loads[5].wait()
    landed(range(CHUNKS))
    for group in range(8):
        aggregate(counts, win, sums, group)
    for half in range(2):
        groups = list(range(4 * half, 4 * half + 4))
        field_of(groups, half, sums, rot, axial, field, acc)

    loads[2].wait()
    loads[3].wait()
    real = [jnp.zeros((8, 128), F32)] * KRYLOV
    imag = [jnp.zeros((8, 128), F32)] * KRYLOV
    for t in range(2):
        upright = jnp.transpose(field[t])
        for start, size in row_pieces(64):
            place = pl.ds(start, size)
            here = upright[start : start + size]
            scale = mie[t, place, :]
            lane = lax.broadcasted_iota(jnp.int32, scale.shape, 1)
            other = pltpu.roll(scale, SPHERES, axis=1)
            scale_real = jnp.where(lane < SPHERES, scale, other)
            scale_imag = jnp.where(lane < SPHERES, other, scale)
            value = basis[last, t, place, :] - (scale_real * here + scale_imag * times_i(here))
            image[t, place, :] = value
            turned = times_i(value)
            for k in range(KRYLOV):
                vector = basis[k, t, place, :]
                real[k] = real[k] + fold(vector * value)
                imag[k] = imag[k] - fold(vector * turned)

    def tile_of(parts):
        rows = [jnp.sum(part, axis=0, keepdims=True) for part in parts]
        return jnp.sum(jnp.concatenate(rows, axis=0), axis=1, keepdims=True)

    def all_sum(call, value):
        steps = ((red_a, a_send, a_recv, group_a, spot), (red_b, b_send, b_recv, group_b, row))
        for store, send_sems, recv_sems, group, index in steps:
            store[call, index] = value
            copies = []
            for n, (other, device) in enumerate(group):
                copy = pltpu.make_async_remote_copy(
                    src_ref=store.at[call, index],
                    dst_ref=store.at[call, index],
                    send_sem=send_sems.at[call, n],
                    recv_sem=recv_sems.at[call, index],
                    device_id=device,
                    device_id_type=MESH,
                )
                copy.start()
                copies.append(copy)
            for other, device in group:
                pltpu.make_async_remote_copy(
                    src_ref=store.at[call, other],
                    dst_ref=store.at[call, other],
                    send_sem=send_sems.at[call, 0],
                    recv_sem=recv_sems.at[call, other],
                    device_id=device,
                    device_id_type=MESH,
                ).wait_recv()
            value = store[call, 0]
            for n in range(1, len(group) + 1):
                value = value + store[call, n]
            for copy in copies:
                copy.wait_send()
        return value

    lane = lax.broadcasted_iota(jnp.int32, (8, 128), 1)
    packed = jnp.where(lane == 0, tile_of(real), jnp.where(lane == 1, tile_of(imag), 0.0))
    dots = all_sum(0, packed) * MEAN_SCALE
    proj_ref[...] = jnp.transpose(dots)[:2]
    for copy in sends:
        copy.wait_send()

    square = jnp.zeros((8, 128), F32)
    for t in range(2):
        for start, size in row_pieces(64):
            place = pl.ds(start, size)
            plain = image[t, place, :]
            turned = jnp.zeros((size, 128), F32)
            for k in range(KRYLOV):
                vector = basis[k, t, place, :]
                plain = plain - dots[k : k + 1, 0:1] * vector
                turned = turned + dots[k : k + 1, 1:2] * vector
            value = plain - times_i(turned)
            image[t, place, :] = value
            square = square + fold(value * value)
    norm_square = jnp.sum(all_sum(1, square)) * MEAN_SCALE
    scale = lax.rsqrt(jnp.full((8, 128), norm_square, F32))[:1]
    for t in range(2):
        out_ref[t] = image[t] * scale


def shards(basis, mie_coeffs, rot_table, axial_table, pair_table, pair_count):
    blocks = basis.shape[1]
    anywhere = pl.BlockSpec(memory_space=pl.ANY)
    return pl.pallas_call(
        kernel,
        out_shape=(
            jax.ShapeDtypeStruct((2, KRYLOV), F32),
            jax.ShapeDtypeStruct((blocks, MODES, 2 * SPHERES), F32),
        ),
        in_specs=[anywhere] * 5 + [pl.BlockSpec(memory_space=pltpu.SMEM)],
        out_specs=(pl.BlockSpec(memory_space=pltpu.VMEM),) * 2,
        scratch_shapes=[
            pltpu.VMEM((KRYLOV, 2, MODES, 128), F32),
            pltpu.VMEM((2, MODES, 128), F32),
            pltpu.VMEM((TABLES, MODES, MODES), BF16),
            pltpu.VMEM((TABLES, 2, MODES, MODES), BF16),
            pltpu.VMEM((128, 3), jnp.int32),
            pltpu.VMEM((128, 128), F32),
            pltpu.VMEM((2, PAD, 128), F32),
            pltpu.VMEM((3, 8, 128), F32),
            pltpu.VMEM((12, 16, ROWS, PAD), BF16),
            pltpu.VMEM((8, 32, ROWS, MODES), BF16),
            pltpu.VMEM((128, MODES), F32),
            pltpu.VMEM((2, 128, PAD), F32),
            pltpu.VMEM((2, MODES, 128), F32),
            pltpu.VMEM((2, 8, 8, 128), F32),
            pltpu.VMEM((2, 16, 8, 128), F32),
            pltpu.SemaphoreType.DMA((6,)),
            pltpu.SemaphoreType.DMA((11 * CHUNKS,)),
            pltpu.SemaphoreType.DMA((12 * CHUNKS,)),
            pltpu.SemaphoreType.DMA((2,)),
            pltpu.SemaphoreType.DMA((2,)),
            pltpu.SemaphoreType.DMA((2, 7)),
            pltpu.SemaphoreType.DMA((2, 8)),
            pltpu.SemaphoreType.DMA((2, 15)),
            pltpu.SemaphoreType.DMA((2, 16)),
        ],
        compiler_params=pltpu.CompilerParams(
            collective_id=0, has_side_effects=True, vmem_limit_bytes=56 * 1024 * 1024
        ),
        name="arnoldi",
    )(basis, mie_coeffs, rot_table, axial_table, pair_table, pair_count)


def solution(mesh):
    placed = (
        P(None, ("blk", "pair"), None, None),
        P(("blk", "pair"), None, None),
        P(),
        P(),
        P("blk", None, None),
        P("blk"),
    )
    return jax.shard_map(
        shards,
        mesh=mesh,
        in_specs=placed,
        out_specs=(P(), P(("blk", "pair"), None, None)),
        check_vma=False,
    )
```

```python
import functools

import jax
import jax.numpy as jnp
from jax import lax
from jax.experimental import pallas as pl
from jax.experimental.pallas import tpu as pltpu
from jax.sharding import PartitionSpec as P

MESH = pl.DeviceIdType.MESH
F32 = jnp.float32
BF16 = jnp.bfloat16
MODES = 510
PAD = 512
KRYLOV = 8
TABLES = 8
BLOCKS = 256
SPHERES = 64
ROWS = 16
CHUNKS = 4
MEAN_SCALE = 1.0 / (BLOCKS * MODES * 2 * SPHERES)

NT = (((1,), (1,)), ((), ()))
NN = (((1,), (0,)), ((), ()))


def dot(left, right, dims):
    return lax.dot_general(left, right, dims, preferred_element_type=F32)


def times_i(value):
    lane = lax.broadcasted_iota(jnp.int32, value.shape, 1)
    turned = pltpu.roll(value, SPHERES, axis=1)
    return jnp.where(lane < SPHERES, -turned, turned)


def fold(value):
    rows = value.shape[0]
    whole = rows // 8 * 8
    total = value[:8]
    for start in range(8, whole, 8):
        total = total + value[start : start + 8]
    if rows > whole:
        rest = value[whole:]
        total = total + jnp.concatenate([rest, jnp.zeros((8 - rest.shape[0], 128), F32)], axis=0)
    return total


def row_pieces(step, total):
    return [(start, min(step, total - start)) for start in range(0, total, step)]


def count_matrix(pairs, member):
    row = lax.broadcasted_iota(jnp.int32, (256, 128), 0)
    g_row = (row >> 5).astype(F32)
    back = ((row >> 4) & 1) == 1
    own = (2 * member + ((row >> 3) & 1)).astype(F32)
    column = (lax.broadcasted_iota(jnp.int32, (192, 128), 0) >> 3).astype(F32)
    total = None
    for off, back_here in ((1, False), (0, True), (1, True), (2, True)):
        a, b, g = (pairs[off, n : n + 1, :] for n in range(3))
        right_table = jnp.where(g_row == g, 1.0, 0.0)
        if back_here:
            hit = jnp.where(back & (own + 8.0 * (2 - off) == b), right_table, 0.0)
            place = jnp.where(column == a + 8.0 * off, 1.0, 0.0)
        else:
            hit = jnp.where((~back) & (own == a), right_table, 0.0)
            place = jnp.where(column == b, 1.0, 0.0)
        term = dot(hit.astype(BF16), place.astype(BF16), NT)
        total = term if total is None else total + term
    same = (lax.broadcasted_iota(jnp.int32, (256, 192), 0) & 7) == (
        lax.broadcasted_iota(jnp.int32, (256, 192), 1) & 7
    )
    return jnp.where(same, total, 0.0).astype(BF16)


def aggregate(counts, win, sums, group):
    halves = []
    for slab in (2 * group, 2 * group + 1):
        part = win[:, slab].reshape(12 * ROWS, PAD)
        halves.append(dot(counts, part, NN).reshape(32, 8, PAD))
    sums[group] = jnp.concatenate(halves, axis=1).astype(BF16)


def chain(g, groups, sums, rot, axial):
    half = len(groups) // 2
    parts = []
    for direction in range(2):
        for imag in range(2):
            for t in range(2):
                for n in groups[imag * half : imag * half + half]:
                    parts.append(sums[n, g * 4 + direction * 2 + t])
    rotation = rot[g]
    first, second = axial[g, 0], axial[g, 1]
    turned = dot(jnp.concatenate(parts, axis=0), rotation, NT).astype(BF16)
    count = turned.shape[0] // 2
    forward, backward = turned[:count], turned[count:]

    def swapped(value):
        return jnp.concatenate([-value[count // 2 :], value[: count // 2]], axis=0)

    moved = dot(forward, first, NT) + dot(swapped(forward), second, NT)
    moved = moved + dot(backward, first, NN) + dot(swapped(backward), second, NN)
    return dot(moved.astype(BF16), rotation, NN)


def field_of(sums, rot, axial, field):
    groups = [half * 4 + imag * 2 + n for imag in range(2) for half in range(2) for n in range(2)]
    total = None
    for g in range(TABLES):
        value = chain(g, groups, sums, rot, axial)
        total = value if total is None else total + value
    for imag in range(2):
        for t in range(2):
            start = (imag * 2 + t) * 64
            field[t, imag * 64 : imag * 64 + 64] = total[start : start + 64]


def kernel(
    basis_hbm, mie_hbm, rot_hbm, axial_hbm, table_hbm, count_ref,
    proj_ref, out_ref,
    basis, mie_raw, mie, rot_raw, axial_raw, rot, axial, table, current, pairs, win, sums, field, mixed, image, red_a, red_b,
    load_sem, send_sem, recv_sem, pair_send, pair_recv, a_send, a_recv, b_send, b_recv,
):
    blk_ways, pair_ways = lax.axis_size("blk"), lax.axis_size("pair")
    blk, member = lax.axis_index("blk"), lax.axis_index("pair")
    core = lax.rem(blk, 2)
    row = blk // 2
    row_ways = blk_ways // 2
    inner = blk + 1 - 2 * core
    outer = lax.rem(blk - 1 + 2 * core + blk_ways, blk_ways)
    right, left, far = (lax.rem(member + n, pair_ways) for n in (1, 3, 2))

    last = KRYLOV - 1
    rows = 2 * MODES
    first_rows = last * rows // 8 * 8
    head, tail = pl.ds(0, first_rows), pl.ds(first_rows, KRYLOV * rows - first_rows)
    load_last = pltpu.make_async_copy(basis_hbm.at[tail], basis.at[tail], load_sem.at[0])
    load_table = pltpu.make_async_copy(table_hbm, table, load_sem.at[1])
    load_rot = pltpu.make_async_copy(rot_hbm, rot_raw, load_sem.at[2])
    load_axial = [
        pltpu.make_async_copy(axial_hbm.at[g], axial_raw.at[g], load_sem.at[5 + g]) for g in range(TABLES)
    ]
    load_rest = pltpu.make_async_copy(basis_hbm.at[head], basis.at[head], load_sem.at[3])
    load_mie = pltpu.make_async_copy(mie_hbm, mie_raw, load_sem.at[4])
    for load in [load_last, load_table, load_rot, *load_axial, load_rest, load_mie]:
        load.start()

    spot = core * pair_ways + member
    group_a = []
    for n in range(1, 2 * pair_ways):
        other = lax.rem(spot + n, 2 * pair_ways)
        group_a.append((other, (2 * row + other // pair_ways, lax.rem(other, pair_ways))))
    group_b = []
    for n in range(1, row_ways):
        other = lax.rem(row + n, row_ways)
        group_b.append((other, (2 * other + core, member)))
    barrier = pltpu.get_barrier_semaphore()
    for device in [(outer, member)] + [d for _, d in group_a] + [d for _, d in group_b]:
        pl.semaphore_signal(barrier, inc=1, device_id=device, device_id_type=MESH)

    load_last.wait()
    current[:, pl.ds(MODES - 6, 8), :] = jnp.zeros((2, 8, 128), F32)
    mine = 4 + member
    for t in range(2):
        current[t, pl.ds(0, MODES), :] = basis[pl.ds(last * rows + t, MODES, stride=2), :]
    flipped = [jnp.transpose(current[t]) for t in range(2)]
    for slab in range(16):
        half, imag, q = slab // 8, slab // 4 % 2, slab % 4
        start = imag * 64 + half * 32 + q * 8
        both = jnp.concatenate([value[start : start + 8] for value in flipped], axis=0)
        win[mine, slab] = both.astype(BF16)
    pl.semaphore_wait(barrier, 1 + len(group_a) + len(group_b))

    width = 16 // CHUNKS
    sends = []

    def send(source_slot, target_slot, chunk, device):
        place = pl.ds(chunk * width, width)
        copy = pltpu.make_async_remote_copy(
            src_ref=win.at[source_slot, place],
            dst_ref=win.at[target_slot, place],
            send_sem=send_sem.at[len(sends)],
            recv_sem=recv_sem.at[target_slot * CHUNKS + chunk],
            device_id=device,
            device_id_type=MESH,
        )
        copy.start()
        sends.append(copy)

    def arrived(slot, chunk):
        place = pl.ds(chunk * width, width)
        pltpu.make_async_remote_copy(
            src_ref=win.at[slot, place],
            dst_ref=win.at[slot, place],
            send_sem=send_sem.at[0],
            recv_sem=recv_sem.at[slot * CHUNKS + chunk],
            device_id=(inner, member),
            device_id_type=MESH,
        ).wait_recv()

    to_inner, to_outer = 8 * core, 8 * (1 - core)
    from_inner, from_outer = 8 * (1 - core), 8 * core
    for chunk in range(CHUNKS):
        send(mine, to_outer + member, chunk, (outer, member))
        send(mine, mine, chunk, (blk, right))
        send(mine, mine, chunk, (blk, left))
        send(mine, to_inner + member, chunk, (inner, member))

    load_table.wait()
    live = lax.broadcasted_iota(jnp.int32, (1, 128), 1) < count_ref[0]
    pairs[1, pl.ds(0, 1), :] = table[0].astype(F32)
    pairs[1, pl.ds(1, 1), :] = table[1].astype(F32)
    pairs[1, pl.ds(2, 1), :] = jnp.where(live, table[2].astype(F32), -1.0)
    pairs[1, pl.ds(3, 5), :] = jnp.zeros((5, 128), F32)
    pair_copies = []
    for n, (slot, device) in enumerate(((2 * core, (inner, member)), (2 - 2 * core, (outer, member)))):
        copy = pltpu.make_async_remote_copy(
            src_ref=pairs.at[1],
            dst_ref=pairs.at[slot],
            send_sem=pair_send.at[n],
            recv_sem=pair_recv.at[n],
            device_id=device,
            device_id_type=MESH,
        )
        copy.start()
        pair_copies.append(copy)

    def forward(chunk):
        for origin, keep_on, device in ((left, 0, right), (right, 1, left)):
            arrived(4 + origin, chunk)
            send(4 + origin, to_outer + origin, chunk, (outer, member))
            if chunk % 2 == keep_on:
                send(4 + origin, 4 + origin, chunk, (blk, device))
            send(4 + origin, to_inner + origin, chunk, (inner, member))

    def forward_far(chunk):
        arrived(4 + far, chunk)
        send(4 + far, to_outer + far, chunk, (outer, member))
        send(4 + far, to_inner + far, chunk, (inner, member))

    def landed(chunks):
        for chunk in chunks:
            for n in range(pair_ways):
                arrived(from_inner + n, chunk)
                arrived(from_outer + n, chunk)

    rot[:, pl.ds(PAD - 16, 16), :] = jnp.zeros((TABLES, 16, PAD), BF16)
    rot[:, :, pl.ds(PAD - 128, 128)] = jnp.zeros((TABLES, PAD, 128), BF16)

    def order_rot():
        load_rot.wait()
        for start, size in row_pieces(32, MODES):
            value = rot_raw[pl.ds(start, size)]
            rot[:, pl.ds(start, size), pl.ds(0, MODES)] = jnp.swapaxes(value, 0, 1)

    def order_axial(g):
        load_axial[g].wait()
        axial[g, :, pl.ds(PAD - 16, 16), :] = jnp.zeros((2, 16, PAD), BF16)
        axial[g, :, :, pl.ds(PAD - 128, 128)] = jnp.zeros((2, PAD, 128), BF16)
        for start, size in row_pieces(64, MODES):
            value = axial_raw[g, pl.ds(start, size)]
            axial[g, :, pl.ds(start, size), pl.ds(0, MODES)] = jnp.swapaxes(value, 0, 1)

    def order_mie():
        load_mie.wait()
        for start, size in row_pieces(32, MODES):
            scale = mie_raw[pl.ds(start, size)].reshape(2 * size, 128)
            lane = lax.broadcasted_iota(jnp.int32, scale.shape, 1)
            other = pltpu.roll(scale, SPHERES, axis=1)
            mie[0, pl.ds(2 * start, 2 * size), :] = jnp.where(lane < SPHERES, scale, other)
            mie[1, pl.ds(2 * start, 2 * size), :] = jnp.where(lane < SPHERES, other, scale)

    order_rot()
    forward(0)
    order_axial(0)
    order_axial(1)
    forward(1)
    forward_far(0)
    order_axial(2)
    order_axial(3)
    forward(2)
    forward_far(1)
    order_axial(4)
    order_axial(5)
    forward(3)
    forward_far(2)
    order_axial(6)
    order_axial(7)
    for copy in pair_copies:
        copy.wait()
    counts = count_matrix(pairs, member)
    order_mie()
    forward_far(3)
    landed(range(CHUNKS))
    for group in range(8):
        aggregate(counts, win, sums, group)
    field_of(sums, rot, axial, field)

    load_rest.wait()
    real = [jnp.zeros((8, 128), F32)] * KRYLOV
    imag = [jnp.zeros((8, 128), F32)] * KRYLOV
    for t in range(2):
        mixed[pl.ds(t, PAD, stride=2), :] = jnp.transpose(field[t])
    for start, size in row_pieces(64, rows):
        place = pl.ds(start, size)
        here = mixed[place, :]
        product = mie[0, place, :] * here + mie[1, place, :] * times_i(here)
        value = basis[pl.ds(last * rows + start, size), :] - product
        image[place, :] = value
        turned = times_i(value)
        for k in range(KRYLOV):
            vector = basis[pl.ds(k * rows + start, size), :]
            real[k] = real[k] + fold(vector * value)
            imag[k] = imag[k] - fold(vector * turned)

    def tile_of(parts):
        rows = [jnp.sum(part, axis=0, keepdims=True) for part in parts]
        return jnp.sum(jnp.concatenate(rows, axis=0), axis=1, keepdims=True)

    def all_sum(call, value):
        steps = ((red_a, a_send, a_recv, group_a, spot), (red_b, b_send, b_recv, group_b, row))
        for store, send_sems, recv_sems, group, index in steps:
            store[call, index] = value
            copies = []
            for n, (other, device) in enumerate(group):
                copy = pltpu.make_async_remote_copy(
                    src_ref=store.at[call, index],
                    dst_ref=store.at[call, index],
                    send_sem=send_sems.at[call, n],
                    recv_sem=recv_sems.at[call, index],
                    device_id=device,
                    device_id_type=MESH,
                )
                copy.start()
                copies.append(copy)
            for other, device in group:
                pltpu.make_async_remote_copy(
                    src_ref=store.at[call, other],
                    dst_ref=store.at[call, other],
                    send_sem=send_sems.at[call, 0],
                    recv_sem=recv_sems.at[call, other],
                    device_id=device,
                    device_id_type=MESH,
                ).wait_recv()
            value = store[call, 0]
            for n in range(1, len(group) + 1):
                value = value + store[call, n]
            sends.extend(copies)
        return value

    lane = lax.broadcasted_iota(jnp.int32, (8, 128), 1)
    packed = jnp.where(lane == 0, tile_of(real), jnp.where(lane == 1, tile_of(imag), 0.0))
    dots = all_sum(0, packed) * MEAN_SCALE
    proj_ref[...] = jnp.transpose(dots)[:2]

    square = jnp.zeros((8, 128), F32)
    for start, size in row_pieces(64, rows):
        place = pl.ds(start, size)
        plain = image[place, :]
        turned = jnp.zeros((size, 128), F32)
        for k in range(KRYLOV):
            vector = basis[pl.ds(k * rows + start, size), :]
            plain = plain - dots[k : k + 1, 0:1] * vector
            turned = turned + dots[k : k + 1, 1:2] * vector
        value = plain - times_i(turned)
        image[place, :] = value
        square = square + fold(value * value)
    norm_square = jnp.sum(all_sum(1, square)) * MEAN_SCALE
    scale = lax.rsqrt(jnp.full((8, 128), norm_square, F32))[:1]
    out_ref[...] = image[...] * scale
    for copy in sends:
        copy.wait_send()


def shards(basis, mie_coeffs, rot_table, axial_table, pair_table, pair_count):
    rows = 2 * MODES
    anywhere = pl.BlockSpec(memory_space=pl.ANY)
    dots, vector = pl.pallas_call(
        kernel,
        out_shape=(
            jax.ShapeDtypeStruct((2, KRYLOV), F32),
            jax.ShapeDtypeStruct((rows, 2 * SPHERES), F32),
        ),
        in_specs=[anywhere] * 5 + [pl.BlockSpec(memory_space=pltpu.SMEM)],
        out_specs=(pl.BlockSpec(memory_space=pltpu.VMEM),) * 2,
        scratch_shapes=[
            pltpu.VMEM((KRYLOV * rows, 128), F32),
            pltpu.VMEM((MODES, 2, 128), F32),
            pltpu.VMEM((2, rows, 128), F32),
            pltpu.VMEM((MODES, TABLES, MODES), BF16),
            pltpu.VMEM((TABLES, MODES, 2, MODES), BF16),
            pltpu.VMEM((TABLES, PAD, PAD), BF16),
            pltpu.VMEM((TABLES, 2, PAD, PAD), BF16),
            pltpu.VMEM((3, 1, 128), jnp.int32),
            pltpu.VMEM((2, PAD, 128), F32),
            pltpu.VMEM((3, 8, 128), F32),
            pltpu.VMEM((12, 16, ROWS, PAD), BF16),
            pltpu.VMEM((8, 32, ROWS, PAD), BF16),
            pltpu.VMEM((2, 128, PAD), F32),
            pltpu.VMEM((2 * PAD, 128), F32),
            pltpu.VMEM((rows, 128), F32),
            pltpu.VMEM((2, 8, 8, 128), F32),
            pltpu.VMEM((2, 16, 8, 128), F32),
            pltpu.SemaphoreType.DMA((13,)),
            pltpu.SemaphoreType.DMA((11 * CHUNKS,)),
            pltpu.SemaphoreType.DMA((12 * CHUNKS,)),
            pltpu.SemaphoreType.DMA((2,)),
            pltpu.SemaphoreType.DMA((2,)),
            pltpu.SemaphoreType.DMA((2, 7)),
            pltpu.SemaphoreType.DMA((2, 8)),
            pltpu.SemaphoreType.DMA((2, 15)),
            pltpu.SemaphoreType.DMA((2, 16)),
        ],
        compiler_params=pltpu.CompilerParams(
            collective_id=0, has_side_effects=True, vmem_limit_bytes=56 * 1024 * 1024
        ),
        name="arnoldi",
    )(
        jnp.transpose(basis, (0, 2, 1, 3)).reshape(KRYLOV * rows, 128),
        jnp.transpose(mie_coeffs, (1, 0, 2)),
        jnp.transpose(rot_table, (1, 0, 2)),
        jnp.transpose(axial_table, (0, 2, 1, 3)),
        jnp.transpose(pair_table, (2, 0, 1)),
        pair_count,
    )
    return dots, jnp.transpose(vector.reshape(MODES, 2, 128), (1, 0, 2))


def solution(mesh):
    placed = (
        P(None, ("blk", "pair"), None, None),
        P(("blk", "pair"), None, None),
        P(),
        P(),
        P("blk", None, None),
        P("blk"),
    )
    return jax.shard_map(
        shards,
        mesh=mesh,
        in_specs=placed,
        out_specs=(P(), P(("blk", "pair"), None, None)),
        check_vma=False,
    )
```

```python
import functools

import jax
import jax.numpy as jnp
from jax import lax
from jax.experimental import pallas as pl
from jax.experimental.pallas import tpu as pltpu
from jax.sharding import PartitionSpec as P

MESH = pl.DeviceIdType.MESH
F32 = jnp.float32
BF16 = jnp.bfloat16
MODES = 510
PAD = 512
KRYLOV = 8
TABLES = 8
BLOCKS = 256
SPHERES = 64
ROWS = 16
CHUNKS = 2
LEAST = 0.01
MOST = 1e37
MEAN_SCALE = 1.0 / (BLOCKS * MODES * 2 * SPHERES)

NT = (((1,), (1,)), ((), ()))
NN = (((1,), (0,)), ((), ()))


def dot(left, right, dims):
    return lax.dot_general(left, right, dims, preferred_element_type=F32)


def times_i(value):
    lane = lax.broadcasted_iota(jnp.int32, value.shape, 1)
    turned = pltpu.roll(value, SPHERES, axis=1)
    return jnp.where(lane < SPHERES, -turned, turned)


def fold(value):
    rows = value.shape[0]
    whole = rows // 8 * 8
    total = value[:8]
    for start in range(8, whole, 8):
        total = total + value[start : start + 8]
    if rows > whole:
        rest = value[whole:]
        total = total + jnp.concatenate([rest, jnp.zeros((8 - rest.shape[0], 128), F32)], axis=0)
    return total


def row_pieces(step, total):
    return [(start, min(step, total - start)) for start in range(0, total, step)]


def count_matrix(pairs, member):
    row = lax.broadcasted_iota(jnp.int32, (256, 128), 0)
    g_row = (row >> 5).astype(F32)
    back = ((row >> 4) & 1) == 1
    own = (2 * member + ((row >> 3) & 1)).astype(F32)
    column = (lax.broadcasted_iota(jnp.int32, (192, 128), 0) >> 3).astype(F32)
    total = None
    for off, back_here in ((1, False), (0, True), (1, True), (2, True)):
        a, b, g = (pairs[off, n : n + 1, :] for n in range(3))
        right_table = jnp.where(g_row == g, 1.0, 0.0)
        if back_here:
            hit = jnp.where(back & (own + 8.0 * (2 - off) == b), right_table, 0.0)
            place = jnp.where(column == a + 8.0 * off, 1.0, 0.0)
        else:
            hit = jnp.where((~back) & (own == a), right_table, 0.0)
            place = jnp.where(column == b, 1.0, 0.0)
        term = dot(hit.astype(BF16), place.astype(BF16), NT)
        total = term if total is None else total + term
    same = (lax.broadcasted_iota(jnp.int32, (256, 192), 0) & 7) == (
        lax.broadcasted_iota(jnp.int32, (256, 192), 1) & 7
    )
    return jnp.where(same, total, 0.0).astype(BF16)


def aggregate(counts, win, sums, group):
    halves = []
    for slab in (2 * group, 2 * group + 1):
        part = win[:, slab].reshape(12 * ROWS, PAD)
        halves.append(dot(counts, part, NN).reshape(32, 8, PAD))
    sums[group] = jnp.concatenate(halves, axis=1).astype(BF16)


def field_of(sums, operators, field):
    groups = [[half * 4 + imag * 2 + n for half in range(2) for n in range(2)] for imag in range(2)]

    def gathered(g, direction):
        parts = []
        for imag in range(2):
            for t in range(2):
                parts.extend(sums[n, g * 4 + direction * 2 + t] for n in groups[imag])
        value = jnp.concatenate(parts, axis=0)
        return value, jnp.concatenate([-value[128:], value[:128]], axis=0)

    total = None
    for g in range(TABLES):
        for direction, dims in ((0, NT), (1, NN)):
            for part, value in enumerate(gathered(g, direction)):
                term = dot(value, operators[g, part], dims)
                total = term if total is None else total + term
    for imag in range(2):
        for t in range(2):
            start = (imag * 2 + t) * 64
            field[t, imag * 64 : imag * 64 + 64] = total[start : start + 64]


def kernel(
    basis_hbm, mie_hbm, rot_hbm, axial_hbm, table_hbm, count_ref,
    proj_ref, out_ref, norm_ref, flag_ref,
    basis, mie_raw, mie, rot_raw, axial_raw, rot, axial, operators, table, current, pairs, win, sums, field, mixed, image, red_a, red_b,
    load_sem, send_sem, recv_sem, pair_send, pair_recv, a_send, a_recv, b_send, b_recv,
):
    blk_ways, pair_ways = lax.axis_size("blk"), lax.axis_size("pair")
    blk, member = lax.axis_index("blk"), lax.axis_index("pair")
    core = lax.rem(blk, 2)
    row = blk // 2
    row_ways = blk_ways // 2
    inner = blk + 1 - 2 * core
    outer = lax.rem(blk - 1 + 2 * core + blk_ways, blk_ways)
    right, left, far = (lax.rem(member + n, pair_ways) for n in (1, 3, 2))

    last = KRYLOV - 1
    rows = 2 * MODES
    first_rows = last * rows // 8 * 8
    head, tail = pl.ds(0, first_rows), pl.ds(first_rows, KRYLOV * rows - first_rows)
    load_last = pltpu.make_async_copy(basis_hbm.at[tail], basis.at[tail], load_sem.at[0])
    load_table = pltpu.make_async_copy(table_hbm, table, load_sem.at[1])
    load_rot = pltpu.make_async_copy(rot_hbm, rot_raw, load_sem.at[2])
    load_axial = [
        pltpu.make_async_copy(axial_hbm.at[g], axial_raw.at[g], load_sem.at[5 + g]) for g in range(TABLES)
    ]
    load_rest = pltpu.make_async_copy(basis_hbm.at[head], basis.at[head], load_sem.at[3])
    load_mie = pltpu.make_async_copy(mie_hbm, mie_raw, load_sem.at[4])
    for load in [load_last, load_table, load_rot, *load_axial, load_rest, load_mie]:
        load.start()

    spot = core * pair_ways + member
    group_a = []
    for n in range(1, 2 * pair_ways):
        other = lax.rem(spot + n, 2 * pair_ways)
        group_a.append((other, (2 * row + other // pair_ways, lax.rem(other, pair_ways))))
    group_b = []
    for n in range(1, row_ways):
        other = lax.rem(row + n, row_ways)
        group_b.append((other, (2 * other + core, member)))
    barrier = pltpu.get_barrier_semaphore()
    for device in [(outer, member)] + [d for _, d in group_a] + [d for _, d in group_b]:
        pl.semaphore_signal(barrier, inc=1, device_id=device, device_id_type=MESH)

    load_last.wait()
    current[:, pl.ds(MODES - 6, 8), :] = jnp.zeros((2, 8, 128), F32)
    mine = 4 + member
    for t in range(2):
        current[t, pl.ds(0, MODES), :] = basis[pl.ds(last * rows + t, MODES, stride=2), :]
    flipped = [jnp.transpose(current[t]) for t in range(2)]
    for slab in range(16):
        half, imag, q = slab // 8, slab // 4 % 2, slab % 4
        start = imag * 64 + half * 32 + q * 8
        both = jnp.concatenate([value[start : start + 8] for value in flipped], axis=0)
        win[mine, slab] = both.astype(BF16)
    pl.semaphore_wait(barrier, 1 + len(group_a) + len(group_b))

    width = 16 // CHUNKS
    sends = []

    def send(source_slot, target_slot, chunk, device):
        place = pl.ds(chunk * width, width)
        copy = pltpu.make_async_remote_copy(
            src_ref=win.at[source_slot, place],
            dst_ref=win.at[target_slot, place],
            send_sem=send_sem.at[len(sends)],
            recv_sem=recv_sem.at[target_slot * CHUNKS + chunk],
            device_id=device,
            device_id_type=MESH,
        )
        copy.start()
        sends.append(copy)

    def arrived(slot, chunk):
        place = pl.ds(chunk * width, width)
        pltpu.make_async_remote_copy(
            src_ref=win.at[slot, place],
            dst_ref=win.at[slot, place],
            send_sem=send_sem.at[0],
            recv_sem=recv_sem.at[slot * CHUNKS + chunk],
            device_id=(inner, member),
            device_id_type=MESH,
        ).wait_recv()

    to_inner, to_outer = 8 * core, 8 * (1 - core)
    from_inner, from_outer = 8 * (1 - core), 8 * core
    for chunk in range(CHUNKS):
        send(mine, to_outer + member, chunk, (outer, member))
        send(mine, mine, chunk, (blk, right))
        send(mine, mine, chunk, (blk, left))
        send(mine, to_inner + member, chunk, (inner, member))

    load_table.wait()
    live = lax.broadcasted_iota(jnp.int32, (1, 128), 1) < count_ref[0]
    pairs[1, pl.ds(0, 1), :] = table[0].astype(F32)
    pairs[1, pl.ds(1, 1), :] = table[1].astype(F32)
    pairs[1, pl.ds(2, 1), :] = jnp.where(live, table[2].astype(F32), -1.0)
    pairs[1, pl.ds(3, 5), :] = jnp.zeros((5, 128), F32)
    pair_copies = []
    for n, (slot, device) in enumerate(((2 * core, (inner, member)), (2 - 2 * core, (outer, member)))):
        copy = pltpu.make_async_remote_copy(
            src_ref=pairs.at[1],
            dst_ref=pairs.at[slot],
            send_sem=pair_send.at[n],
            recv_sem=pair_recv.at[n],
            device_id=device,
            device_id_type=MESH,
        )
        copy.start()
        pair_copies.append(copy)

    def forward(chunk):
        for origin, keep_on, device in ((left, 0, right), (right, 1, left)):
            arrived(4 + origin, chunk)
            send(4 + origin, to_outer + origin, chunk, (outer, member))
            if chunk % 2 == keep_on:
                send(4 + origin, 4 + origin, chunk, (blk, device))
            send(4 + origin, to_inner + origin, chunk, (inner, member))

    def forward_far(chunk):
        arrived(4 + far, chunk)
        send(4 + far, to_outer + far, chunk, (outer, member))
        send(4 + far, to_inner + far, chunk, (inner, member))

    def landed(chunks):
        for chunk in chunks:
            for n in range(pair_ways):
                arrived(from_inner + n, chunk)
                arrived(from_outer + n, chunk)

    rot[:, pl.ds(PAD - 16, 16), :] = jnp.zeros((TABLES, 16, PAD), BF16)
    rot[:, :, pl.ds(PAD - 128, 128)] = jnp.zeros((TABLES, PAD, 128), BF16)

    def order_rot():
        load_rot.wait()
        for start, size in row_pieces(32, MODES):
            value = rot_raw[pl.ds(start, size)]
            rot[:, pl.ds(start, size), pl.ds(0, MODES)] = jnp.swapaxes(value, 0, 1)

    def operator(g):
        load_axial[g].wait()
        slot = g % 2
        for start, size in row_pieces(64, MODES):
            value = axial_raw[g, pl.ds(start, size)]
            axial[slot, :, pl.ds(start, size), pl.ds(0, MODES)] = jnp.swapaxes(value, 0, 1)
        rotation = rot[g]
        flipped = jnp.transpose(rotation)
        for part in range(2):
            moved = dot(axial[slot, part], rotation, NN).astype(BF16)
            operators[g, part] = dot(flipped, moved, NN).astype(BF16)

    def gram():
        lane = lax.broadcasted_iota(jnp.int32, (1, 128), 1)
        lines = []
        for j in range(KRYLOV):
            real = [jnp.zeros((8, 128), F32)] * KRYLOV
            imag = [jnp.zeros((8, 128), F32)] * KRYLOV
            for start, size in row_pieces(64, rows):
                one = basis[pl.ds(j * rows + start, size), :]
                turned = times_i(one)
                for k in range(j, KRYLOV):
                    other = basis[pl.ds(k * rows + start, size), :]
                    real[k] = real[k] + fold(one * other)
                    if k > j:
                        imag[k] = imag[k] + fold(turned * other)
            line = jnp.zeros((1, 128), F32)
            for k in range(j, KRYLOV):
                line = jnp.where(lane == 8 + k, jnp.sum(real[k]), line)
                if k > j:
                    line = jnp.where(lane == 16 + k, jnp.sum(imag[k]), line)
            lines.append(line)
        return jnp.concatenate(lines, axis=0)

    def order_mie():
        load_mie.wait()
        for start, size in row_pieces(32, MODES):
            scale = mie_raw[pl.ds(start, size)].reshape(2 * size, 128)
            lane = lax.broadcasted_iota(jnp.int32, scale.shape, 1)
            other = pltpu.roll(scale, SPHERES, axis=1)
            mie[0, pl.ds(2 * start, 2 * size), :] = jnp.where(lane < SPHERES, scale, other)
            mie[1, pl.ds(2 * start, 2 * size), :] = jnp.where(lane < SPHERES, other, scale)

    axial[:, :, pl.ds(PAD - 16, 16), :] = jnp.zeros((2, 2, 16, PAD), BF16)
    axial[:, :, :, pl.ds(PAD - 128, 128)] = jnp.zeros((2, 2, PAD, 128), BF16)
    order_rot()
    operator(0)
    operator(1)
    forward(0)
    operator(2)
    operator(3)
    forward(1)
    operator(4)
    forward_far(0)
    operator(5)
    forward_far(1)
    operator(6)
    operator(7)
    for copy in pair_copies:
        copy.wait()
    counts = count_matrix(pairs, member)
    order_mie()
    load_rest.wait()
    packed_gram = gram()
    landed(range(CHUNKS))
    for group in range(8):
        aggregate(counts, win, sums, group)
    field_of(sums, operators, field)

    real = [jnp.zeros((8, 128), F32)] * KRYLOV
    imag = [jnp.zeros((8, 128), F32)] * KRYLOV
    square = jnp.zeros((8, 128), F32)
    for t in range(2):
        mixed[pl.ds(t, PAD, stride=2), :] = jnp.transpose(field[t])
    for start, size in row_pieces(64, rows):
        place = pl.ds(start, size)
        here = mixed[place, :]
        product = mie[0, place, :] * here + mie[1, place, :] * times_i(here)
        value = basis[pl.ds(last * rows + start, size), :] - product
        image[place, :] = value
        turned = times_i(value)
        square = square + fold(value * value)
        for k in range(KRYLOV):
            vector = basis[pl.ds(k * rows + start, size), :]
            real[k] = real[k] + fold(vector * value)
            imag[k] = imag[k] - fold(vector * turned)

    def tile_of(parts):
        rows = [jnp.sum(part, axis=0, keepdims=True) for part in parts]
        return jnp.sum(jnp.concatenate(rows, axis=0), axis=1, keepdims=True)

    def all_sum(call, value):
        steps = ((red_a, a_send, a_recv, group_a, spot), (red_b, b_send, b_recv, group_b, row))
        for store, send_sems, recv_sems, group, index in steps:
            store[call, index] = value
            copies = []
            for n, (other, device) in enumerate(group):
                copy = pltpu.make_async_remote_copy(
                    src_ref=store.at[call, index],
                    dst_ref=store.at[call, index],
                    send_sem=send_sems.at[call, n],
                    recv_sem=recv_sems.at[call, index],
                    device_id=device,
                    device_id_type=MESH,
                )
                copy.start()
                copies.append(copy)
            for copy in sends:
                copy.wait_send()
            sends.clear()
            for other, device in group:
                pltpu.make_async_remote_copy(
                    src_ref=store.at[call, other],
                    dst_ref=store.at[call, other],
                    send_sem=send_sems.at[call, 0],
                    recv_sem=recv_sems.at[call, other],
                    device_id=device,
                    device_id_type=MESH,
                ).wait_recv()
            value = store[call, 0]
            for n in range(1, len(group) + 1):
                value = value + store[call, n]
            sends.extend(copies)
        return value

    lane = lax.broadcasted_iota(jnp.int32, (8, 128), 1)
    packed = jnp.where(lane == 0, tile_of(real), jnp.where(lane == 1, tile_of(imag), packed_gram))
    packed = jnp.where(lane == 2, jnp.sum(square) * 0.125, packed)
    reduced = all_sum(0, packed)
    dots = reduced * MEAN_SCALE
    turned_dots = jnp.transpose(jnp.concatenate([dots, jnp.zeros((120, 128), F32)], axis=0))
    proj_ref[...] = turned_dots[:2, :KRYLOV]

    first, second = jnp.where(lane < KRYLOV, turned_dots[0:1], 0.0), jnp.where(lane < KRYLOV, turned_dots[1:2], 0.0)
    c_real, c_imag = dots[:, 0:1], dots[:, 1:2]
    weight = jnp.where(lane == lax.broadcasted_iota(jnp.int32, (8, 128), 0), 1.0, 2.0)
    gram_real, gram_imag = pltpu.roll(reduced, 120, axis=1), pltpu.roll(reduced, 112, axis=1)
    form = (c_real * first + c_imag * second) * gram_real - (c_real * second - c_imag * first) * gram_imag
    quadratic = jnp.sum(jnp.where(lane < KRYLOV, weight * form, 0.0)) * MEAN_SCALE
    linear = 2.0 * jnp.sum(jnp.where(lane < 2, dots * dots, 0.0))
    constant = jnp.sum(jnp.where(lane == 2, dots, 0.0))
    norm_square = constant - linear + quadratic
    fine = (norm_square > LEAST * (constant + linear + quadratic)) & (norm_square < MOST)
    norm_ref[0] = norm_square
    flag_ref[0] = jnp.where(fine, 0, 1)

    for start, size in row_pieces(64, rows):
        place = pl.ds(start, size)
        plain = image[place, :]
        turned = jnp.zeros((size, 128), F32)
        for k in range(KRYLOV):
            vector = basis[pl.ds(k * rows + start, size), :]
            plain = plain - dots[k : k + 1, 0:1] * vector
            turned = turned + dots[k : k + 1, 1:2] * vector
        out_ref[place, :] = plain - times_i(turned)
    for copy in sends:
        copy.wait_send()


def shards(basis, mie_coeffs, rot_table, axial_table, pair_table, pair_count):
    rows = 2 * MODES
    anywhere = pl.BlockSpec(memory_space=pl.ANY)
    dots, vector, norm_square, flag = pl.pallas_call(
        kernel,
        out_shape=(
            jax.ShapeDtypeStruct((2, KRYLOV), F32),
            jax.ShapeDtypeStruct((rows, 2 * SPHERES), F32),
            jax.ShapeDtypeStruct((1,), F32),
            jax.ShapeDtypeStruct((1,), jnp.int32),
        ),
        in_specs=[anywhere] * 5 + [pl.BlockSpec(memory_space=pltpu.SMEM)],
        out_specs=(pl.BlockSpec(memory_space=pltpu.VMEM),) * 2 + (pl.BlockSpec(memory_space=pltpu.SMEM),) * 2,
        scratch_shapes=[
            pltpu.VMEM((KRYLOV * rows, 128), F32),
            pltpu.VMEM((MODES, 2, 128), F32),
            pltpu.VMEM((2, rows, 128), F32),
            pltpu.VMEM((MODES, TABLES, MODES), BF16),
            pltpu.VMEM((TABLES, MODES, 2, MODES), BF16),
            pltpu.VMEM((TABLES, PAD, PAD), BF16),
            pltpu.VMEM((2, 2, PAD, PAD), BF16),
            pltpu.VMEM((TABLES, 2, PAD, PAD), BF16),
            pltpu.VMEM((3, 1, 128), jnp.int32),
            pltpu.VMEM((2, PAD, 128), F32),
            pltpu.VMEM((3, 8, 128), F32),
            pltpu.VMEM((12, 16, ROWS, PAD), BF16),
            pltpu.VMEM((8, 32, ROWS, PAD), BF16),
            pltpu.VMEM((2, 128, PAD), F32),
            pltpu.VMEM((2 * PAD, 128), F32),
            pltpu.VMEM((rows, 128), F32),
            pltpu.VMEM((1, 8, 8, 128), F32),
            pltpu.VMEM((1, 16, 8, 128), F32),
            pltpu.SemaphoreType.DMA((13,)),
            pltpu.SemaphoreType.DMA((11 * CHUNKS,)),
            pltpu.SemaphoreType.DMA((12 * CHUNKS,)),
            pltpu.SemaphoreType.DMA((2,)),
            pltpu.SemaphoreType.DMA((2,)),
            pltpu.SemaphoreType.DMA((1, 7)),
            pltpu.SemaphoreType.DMA((1, 8)),
            pltpu.SemaphoreType.DMA((1, 15)),
            pltpu.SemaphoreType.DMA((1, 16)),
        ],
        compiler_params=pltpu.CompilerParams(
            collective_id=0, has_side_effects=True, vmem_limit_bytes=56 * 1024 * 1024
        ),
        name="arnoldi",
    )(
        jnp.transpose(basis, (0, 2, 1, 3)).reshape(KRYLOV * rows, 128),
        jnp.transpose(mie_coeffs, (1, 0, 2)),
        jnp.transpose(rot_table, (1, 0, 2)),
        jnp.transpose(axial_table, (0, 2, 1, 3)),
        jnp.transpose(pair_table, (2, 0, 1)),
        pair_count,
    )
    def direct(vector, norm_square):
        return lax.psum(jnp.sum(vector * vector), ("blk", "pair")) * MEAN_SCALE

    norm_square = lax.cond(flag[0] != 0, direct, lambda vector, norm_square: norm_square, vector, norm_square[0])
    vector = vector * lax.rsqrt(norm_square)
    return dots, jnp.transpose(vector.reshape(MODES, 2, 128), (1, 0, 2))


def solution(mesh):
    placed = (
        P(None, ("blk", "pair"), None, None),
        P(("blk", "pair"), None, None),
        P(),
        P(),
        P("blk", None, None),
        P("blk"),
    )
    return jax.shard_map(
        shards,
        mesh=mesh,
        in_specs=placed,
        out_specs=(P(), P(("blk", "pair"), None, None)),
        check_vma=False,
    )
```

```python
import functools

import jax
import jax.numpy as jnp
from jax import lax
from jax.experimental import pallas as pl
from jax.experimental.pallas import tpu as pltpu
from jax.sharding import PartitionSpec as P

MESH = pl.DeviceIdType.MESH
F32 = jnp.float32
BF16 = jnp.bfloat16
MODES = 510
PAD = 512
KRYLOV = 8
TABLES = 8
BLOCKS = 256
SPHERES = 64
ROWS = 16
CHUNKS = 2
LEAST = 0.01
MOST = 1e37
MEAN_SCALE = 1.0 / (BLOCKS * MODES * 2 * SPHERES)

NT = (((1,), (1,)), ((), ()))
NN = (((1,), (0,)), ((), ()))


def dot(left, right, dims):
    return lax.dot_general(left, right, dims, preferred_element_type=F32)


def times_i(value):
    lane = lax.broadcasted_iota(jnp.int32, value.shape, 1)
    turned = pltpu.roll(value, SPHERES, axis=1)
    return jnp.where(lane < SPHERES, -turned, turned)


def fold(value):
    rows = value.shape[0]
    whole = rows // 8 * 8
    total = value[:8]
    for start in range(8, whole, 8):
        total = total + value[start : start + 8]
    if rows > whole:
        rest = value[whole:]
        total = total + jnp.concatenate([rest, jnp.zeros((8 - rest.shape[0], 128), F32)], axis=0)
    return total


def row_pieces(step, total):
    return [(start, min(step, total - start)) for start in range(0, total, step)]


def count_matrix(pairs, member):
    row = lax.broadcasted_iota(jnp.int32, (256, 128), 0)
    g_row = (row >> 5).astype(F32)
    back = ((row >> 4) & 1) == 1
    own = (2 * member + ((row >> 3) & 1)).astype(F32)
    column = (lax.broadcasted_iota(jnp.int32, (192, 128), 0) >> 3).astype(F32)
    total = None
    for off, back_here in ((1, False), (0, True), (1, True), (2, True)):
        a, b, g = (pairs[off, n : n + 1, :] for n in range(3))
        right_table = jnp.where(g_row == g, 1.0, 0.0)
        if back_here:
            hit = jnp.where(back & (own + 8.0 * (2 - off) == b), right_table, 0.0)
            place = jnp.where(column == a + 8.0 * off, 1.0, 0.0)
        else:
            hit = jnp.where((~back) & (own == a), right_table, 0.0)
            place = jnp.where(column == b, 1.0, 0.0)
        term = dot(hit.astype(BF16), place.astype(BF16), NT)
        total = term if total is None else total + term
    same = (lax.broadcasted_iota(jnp.int32, (256, 192), 0) & 7) == (
        lax.broadcasted_iota(jnp.int32, (256, 192), 1) & 7
    )
    return jnp.where(same, total, 0.0).astype(BF16)


def aggregate(counts, win, sums, group):
    halves = []
    for slab in (2 * group, 2 * group + 1):
        part = win[:, slab].reshape(12 * ROWS, PAD)
        halves.append(dot(counts, part, NN).reshape(32, 8, PAD))
    sums[group] = jnp.concatenate(halves, axis=1).astype(BF16)


def field_of(sums, operators, field):
    groups = [[half * 4 + imag * 2 + n for half in range(2) for n in range(2)] for imag in range(2)]

    def gathered(g, direction):
        parts = []
        for imag in range(2):
            for t in range(2):
                parts.extend(sums[n, g * 4 + direction * 2 + t] for n in groups[imag])
        value = jnp.concatenate(parts, axis=0)
        return value, jnp.concatenate([-value[128:], value[:128]], axis=0)

    total = None
    for g in range(TABLES):
        for direction, dims in ((0, NT), (1, NN)):
            for part, value in enumerate(gathered(g, direction)):
                term = dot(value, operators[g, part], dims)
                total = term if total is None else total + term
    for imag in range(2):
        for t in range(2):
            start = (imag * 2 + t) * 64
            field[t, imag * 64 : imag * 64 + 64] = total[start : start + 64]


def kernel(
    basis_hbm, mie_hbm, rot_hbm, axial_hbm, table_hbm, count_ref,
    proj_ref, out_ref, norm_ref, flag_ref,
    basis, mie_raw, mie, rot_raw, axial_raw, rot, axial, operators, table, current, pairs, win, sums, field, mixed, image, red_a, red_b,
    load_sem, send_sem, recv_sem, pair_send, pair_recv, a_send, a_recv, b_send, b_recv,
):
    blk_ways, pair_ways = lax.axis_size("blk"), lax.axis_size("pair")
    blk, member = lax.axis_index("blk"), lax.axis_index("pair")
    core = lax.rem(blk, 2)
    row = blk // 2
    row_ways = blk_ways // 2
    inner = blk + 1 - 2 * core
    outer = lax.rem(blk - 1 + 2 * core + blk_ways, blk_ways)
    right, left, far = (lax.rem(member + n, pair_ways) for n in (1, 3, 2))

    last = KRYLOV - 1
    rows = 2 * MODES
    first_rows = last * rows // 8 * 8
    head, tail = pl.ds(0, first_rows), pl.ds(first_rows, KRYLOV * rows - first_rows)
    load_last = pltpu.make_async_copy(basis_hbm.at[tail], basis.at[tail], load_sem.at[0])
    load_table = pltpu.make_async_copy(table_hbm, table, load_sem.at[1])
    load_rot = pltpu.make_async_copy(rot_hbm, rot_raw, load_sem.at[2])
    load_axial = [
        pltpu.make_async_copy(axial_hbm.at[g], axial_raw.at[g], load_sem.at[5 + g]) for g in range(TABLES)
    ]
    load_rest = pltpu.make_async_copy(basis_hbm.at[head], basis.at[head], load_sem.at[3])
    load_mie = pltpu.make_async_copy(mie_hbm, mie_raw, load_sem.at[4])
    for load in [load_last, load_table, load_rot, *load_axial[:4], load_rest, *load_axial[4:], load_mie]:
        load.start()

    spot = core * pair_ways + member
    group_a = []
    for n in (2, 6, 1, 3, 5, 7, 4):
        other = lax.rem(spot + n, 2 * pair_ways)
        group_a.append((other, (2 * row + other // pair_ways, lax.rem(other, pair_ways))))
    group_b = []
    high, low = row // 4, lax.rem(row, 4)
    steps = [(n, m) for n in range(4) for m in range(4) if n or m]
    for n, m in sorted(steps, key=lambda step: -min(step[0], 4 - step[0]) - min(step[1], 4 - step[1])):
        other = 4 * lax.rem(high + n, 4) + lax.rem(low + m, 4)
        group_b.append((other, (2 * other + core, member)))
    barrier = pltpu.get_barrier_semaphore()
    for device in [(outer, member)] + [d for _, d in group_a] + [d for _, d in group_b]:
        pl.semaphore_signal(barrier, inc=1, device_id=device, device_id_type=MESH)

    load_last.wait()
    current[:, pl.ds(MODES - 6, 8), :] = jnp.zeros((2, 8, 128), F32)
    mine = 4 + member
    for t in range(2):
        current[t, pl.ds(0, MODES), :] = basis[pl.ds(last * rows + t, MODES, stride=2), :]
    flipped = [jnp.transpose(current[t]) for t in range(2)]
    for slab in range(16):
        half, imag, q = slab // 8, slab // 4 % 2, slab % 4
        start = imag * 64 + half * 32 + q * 8
        both = jnp.concatenate([value[start : start + 8] for value in flipped], axis=0)
        win[mine, slab] = both.astype(BF16)
    pl.semaphore_wait(barrier, 1 + len(group_a) + len(group_b))

    width = 16 // CHUNKS
    sends = []

    def send(source_slot, target_slot, chunk, device):
        place = pl.ds(chunk * width, width)
        copy = pltpu.make_async_remote_copy(
            src_ref=win.at[source_slot, place],
            dst_ref=win.at[target_slot, place],
            send_sem=send_sem.at[len(sends)],
            recv_sem=recv_sem.at[target_slot * CHUNKS + chunk],
            device_id=device,
            device_id_type=MESH,
        )
        copy.start()
        sends.append(copy)

    def arrived(slot, chunk):
        place = pl.ds(chunk * width, width)
        pltpu.make_async_remote_copy(
            src_ref=win.at[slot, place],
            dst_ref=win.at[slot, place],
            send_sem=send_sem.at[0],
            recv_sem=recv_sem.at[slot * CHUNKS + chunk],
            device_id=(inner, member),
            device_id_type=MESH,
        ).wait_recv()

    to_inner, to_outer = 8 * core, 8 * (1 - core)
    from_inner, from_outer = 8 * (1 - core), 8 * core
    for chunk in range(CHUNKS):
        send(mine, to_outer + member, chunk, (outer, member))
        send(mine, mine, chunk, (blk, right))
        send(mine, mine, chunk, (blk, left))
        send(mine, to_inner + member, chunk, (inner, member))

    load_table.wait()
    live = lax.broadcasted_iota(jnp.int32, (1, 128), 1) < count_ref[0]
    pairs[1, pl.ds(0, 1), :] = table[0].astype(F32)
    pairs[1, pl.ds(1, 1), :] = table[1].astype(F32)
    pairs[1, pl.ds(2, 1), :] = jnp.where(live, table[2].astype(F32), -1.0)
    pairs[1, pl.ds(3, 5), :] = jnp.zeros((5, 128), F32)
    pair_copies = []
    for n, (slot, device) in enumerate(((2 * core, (inner, member)), (2 - 2 * core, (outer, member)))):
        copy = pltpu.make_async_remote_copy(
            src_ref=pairs.at[1],
            dst_ref=pairs.at[slot],
            send_sem=pair_send.at[n],
            recv_sem=pair_recv.at[n],
            device_id=device,
            device_id_type=MESH,
        )
        copy.start()
        pair_copies.append(copy)

    def forward(chunk):
        for origin, keep_on, device in ((left, 0, right), (right, 1, left)):
            arrived(4 + origin, chunk)
            send(4 + origin, to_outer + origin, chunk, (outer, member))
            if chunk % 2 == keep_on:
                send(4 + origin, 4 + origin, chunk, (blk, device))
            send(4 + origin, to_inner + origin, chunk, (inner, member))

    def forward_far(chunk):
        arrived(4 + far, chunk)
        send(4 + far, to_outer + far, chunk, (outer, member))
        send(4 + far, to_inner + far, chunk, (inner, member))

    def landed(chunks):
        for chunk in chunks:
            for n in range(pair_ways):
                arrived(from_inner + n, chunk)
                arrived(from_outer + n, chunk)

    rot[:, pl.ds(PAD - 16, 16), :] = jnp.zeros((TABLES, 16, PAD), BF16)
    rot[:, :, pl.ds(PAD - 128, 128)] = jnp.zeros((TABLES, PAD, 128), BF16)

    def order_rot():
        load_rot.wait()
        for start, size in row_pieces(32, MODES):
            value = rot_raw[pl.ds(start, size)]
            rot[:, pl.ds(start, size), pl.ds(0, MODES)] = jnp.swapaxes(value, 0, 1)

    def order_axial(g):
        for start, size in row_pieces(64, MODES):
            value = axial_raw[g, pl.ds(start, size)]
            axial[g % 2, :, pl.ds(start, size), pl.ds(0, MODES)] = jnp.swapaxes(value, 0, 1)

    def operator(g):
        rotation = rot[g]
        flipped = jnp.transpose(rotation)
        for part in range(2):
            moved = dot(axial[g % 2, part], rotation, NN).astype(BF16)
            operators[g, part] = dot(flipped, moved, NN).astype(BF16)

    lines = []

    def gram_line(j):
        lane = lax.broadcasted_iota(jnp.int32, (1, 128), 1)
        real = [jnp.zeros((8, 128), F32)] * KRYLOV
        imag = [jnp.zeros((8, 128), F32)] * KRYLOV
        for start, size in row_pieces(64, rows):
            one = basis[pl.ds(j * rows + start, size), :]
            turned = times_i(one)
            for k in range(j, KRYLOV):
                other = basis[pl.ds(k * rows + start, size), :]
                real[k] = real[k] + fold(one * other)
                if k > j:
                    imag[k] = imag[k] + fold(turned * other)
        line = jnp.zeros((1, 128), F32)
        for k in range(j, KRYLOV):
            line = jnp.where(lane == 8 + k, jnp.sum(real[k]), line)
            if k > j:
                line = jnp.where(lane == 16 + k, jnp.sum(imag[k]), line)
        lines.append(line)

    def order_mie():
        for start, size in row_pieces(32, MODES):
            scale = mie_raw[pl.ds(start, size)].reshape(2 * size, 128)
            lane = lax.broadcasted_iota(jnp.int32, scale.shape, 1)
            other = pltpu.roll(scale, SPHERES, axis=1)
            mie[0, pl.ds(2 * start, 2 * size), :] = jnp.where(lane < SPHERES, scale, other)
            mie[1, pl.ds(2 * start, 2 * size), :] = jnp.where(lane < SPHERES, other, scale)

    axial[:, :, pl.ds(PAD - 16, 16), :] = jnp.zeros((2, 2, 16, PAD), BF16)
    axial[:, :, :, pl.ds(PAD - 128, 128)] = jnp.zeros((2, 2, PAD, 128), BF16)
    order_rot()
    load_axial[0].wait()
    order_axial(0)
    load_axial[1].wait()
    order_axial(1)
    operator(0)
    load_axial[2].wait()
    order_axial(2)
    operator(1)
    forward(0)
    load_axial[3].wait()
    load_rest.wait()
    order_axial(3)
    operator(2)
    gram_line(0)
    load_axial[4].wait()
    order_axial(4)
    operator(3)
    gram_line(1)
    forward(1)
    load_axial[5].wait()
    order_axial(5)
    operator(4)
    gram_line(2)
    forward_far(0)
    load_axial[6].wait()
    order_axial(6)
    operator(5)
    gram_line(3)
    forward_far(1)
    load_axial[7].wait()
    load_mie.wait()
    for copy in pair_copies:
        copy.wait()
    order_axial(7)
    operator(6)
    gram_line(4)
    gram_line(5)
    counts = count_matrix(pairs, member)
    operator(7)
    gram_line(6)
    gram_line(7)
    order_mie()
    packed_gram = jnp.concatenate(lines, axis=0)
    landed(range(CHUNKS))
    for group in range(8):
        aggregate(counts, win, sums, group)
    field_of(sums, operators, field)

    real = [jnp.zeros((8, 128), F32)] * KRYLOV
    imag = [jnp.zeros((8, 128), F32)] * KRYLOV
    square = jnp.zeros((8, 128), F32)
    for t in range(2):
        mixed[pl.ds(t, PAD, stride=2), :] = jnp.transpose(field[t])
    for start, size in row_pieces(64, rows):
        place = pl.ds(start, size)
        here = mixed[place, :]
        product = mie[0, place, :] * here + mie[1, place, :] * times_i(here)
        value = basis[pl.ds(last * rows + start, size), :] - product
        image[place, :] = value
        turned = times_i(value)
        square = square + fold(value * value)
        for k in range(KRYLOV):
            vector = basis[pl.ds(k * rows + start, size), :]
            real[k] = real[k] + fold(vector * value)
            imag[k] = imag[k] - fold(vector * turned)

    def tile_of(parts):
        rows = [jnp.sum(part, axis=0, keepdims=True) for part in parts]
        return jnp.sum(jnp.concatenate(rows, axis=0), axis=1, keepdims=True)

    def all_sum(call, value):
        steps = ((red_a, a_send, a_recv, group_a, spot), (red_b, b_send, b_recv, group_b, row))
        for store, send_sems, recv_sems, group, index in steps:
            store[call, index] = value
            copies = []
            for n, (other, device) in enumerate(group):
                copy = pltpu.make_async_remote_copy(
                    src_ref=store.at[call, index],
                    dst_ref=store.at[call, index],
                    send_sem=send_sems.at[call, n],
                    recv_sem=recv_sems.at[call, index],
                    device_id=device,
                    device_id_type=MESH,
                )
                copy.start()
                copies.append(copy)
            for copy in sends:
                copy.wait_send()
            sends.clear()
            for other, device in group:
                pltpu.make_async_remote_copy(
                    src_ref=store.at[call, other],
                    dst_ref=store.at[call, other],
                    send_sem=send_sems.at[call, 0],
                    recv_sem=recv_sems.at[call, other],
                    device_id=device,
                    device_id_type=MESH,
                ).wait_recv()
            value = store[call, 0]
            for n in range(1, len(group) + 1):
                value = value + store[call, n]
            sends.extend(copies)
        return value

    lane = lax.broadcasted_iota(jnp.int32, (8, 128), 1)
    packed = jnp.where(lane == 0, tile_of(real), jnp.where(lane == 1, tile_of(imag), packed_gram))
    packed = jnp.where(lane == 2, jnp.sum(square) * 0.125, packed)
    reduced = all_sum(0, packed)
    dots = reduced * MEAN_SCALE
    turned_dots = jnp.transpose(jnp.concatenate([dots, jnp.zeros((120, 128), F32)], axis=0))
    proj_ref[...] = jnp.transpose(jnp.concatenate([reduced, jnp.zeros((120, 128), F32)], axis=0))[:2, :KRYLOV]

    first, second = jnp.where(lane < KRYLOV, turned_dots[0:1], 0.0), jnp.where(lane < KRYLOV, turned_dots[1:2], 0.0)
    c_real, c_imag = dots[:, 0:1], dots[:, 1:2]
    weight = jnp.where(lane == lax.broadcasted_iota(jnp.int32, (8, 128), 0), 1.0, 2.0)
    gram_real, gram_imag = pltpu.roll(reduced, 120, axis=1), pltpu.roll(reduced, 112, axis=1)
    form = (c_real * first + c_imag * second) * gram_real - (c_real * second - c_imag * first) * gram_imag
    quadratic = jnp.sum(jnp.where(lane < KRYLOV, weight * form, 0.0)) * MEAN_SCALE
    linear = 2.0 * jnp.sum(jnp.where(lane < 2, dots * dots, 0.0))
    constant = jnp.sum(jnp.where(lane == 2, dots, 0.0))
    norm_square = constant - linear + quadratic
    fine = (norm_square > LEAST * (constant + linear + quadratic)) & (norm_square < MOST)
    norm_ref[0] = norm_square
    flag_ref[0] = jnp.where(fine, 0, 1)

    for start, size in row_pieces(64, rows):
        place = pl.ds(start, size)
        plain = image[place, :]
        turned = jnp.zeros((size, 128), F32)
        for k in range(KRYLOV):
            vector = basis[pl.ds(k * rows + start, size), :]
            plain = plain - dots[k : k + 1, 0:1] * vector
            turned = turned + dots[k : k + 1, 1:2] * vector
        out_ref[place, :] = plain - times_i(turned)
    for copy in sends:
        copy.wait_send()


def shards(basis, mie_coeffs, rot_table, axial_table, pair_table, pair_count):
    rows = 2 * MODES
    anywhere = pl.BlockSpec(memory_space=pl.ANY)
    dots, vector, norm_square, flag = pl.pallas_call(
        kernel,
        out_shape=(
            jax.ShapeDtypeStruct((2, KRYLOV), F32),
            jax.ShapeDtypeStruct((rows, 2 * SPHERES), F32),
            jax.ShapeDtypeStruct((1,), F32),
            jax.ShapeDtypeStruct((1,), jnp.int32),
        ),
        in_specs=[anywhere] * 5 + [pl.BlockSpec(memory_space=pltpu.SMEM)],
        out_specs=(pl.BlockSpec(memory_space=pltpu.VMEM),) * 2 + (pl.BlockSpec(memory_space=pltpu.SMEM),) * 2,
        scratch_shapes=[
            pltpu.VMEM((KRYLOV * rows, 128), F32),
            pltpu.VMEM((MODES, 2, 128), F32),
            pltpu.VMEM((2, rows, 128), F32),
            pltpu.VMEM((MODES, TABLES, MODES), BF16),
            pltpu.VMEM((TABLES, MODES, 2, MODES), BF16),
            pltpu.VMEM((TABLES, PAD, PAD), BF16),
            pltpu.VMEM((2, 2, PAD, PAD), BF16),
            pltpu.VMEM((TABLES, 2, PAD, PAD), BF16),
            pltpu.VMEM((3, 1, 128), jnp.int32),
            pltpu.VMEM((2, PAD, 128), F32),
            pltpu.VMEM((3, 8, 128), F32),
            pltpu.VMEM((12, 16, ROWS, PAD), BF16),
            pltpu.VMEM((8, 32, ROWS, PAD), BF16),
            pltpu.VMEM((2, 128, PAD), F32),
            pltpu.VMEM((2 * PAD, 128), F32),
            pltpu.VMEM((rows, 128), F32),
            pltpu.VMEM((1, 8, 8, 128), F32),
            pltpu.VMEM((1, 16, 8, 128), F32),
            pltpu.SemaphoreType.DMA((13,)),
            pltpu.SemaphoreType.DMA((11 * CHUNKS,)),
            pltpu.SemaphoreType.DMA((12 * CHUNKS,)),
            pltpu.SemaphoreType.DMA((2,)),
            pltpu.SemaphoreType.DMA((2,)),
            pltpu.SemaphoreType.DMA((1, 7)),
            pltpu.SemaphoreType.DMA((1, 8)),
            pltpu.SemaphoreType.DMA((1, 15)),
            pltpu.SemaphoreType.DMA((1, 16)),
        ],
        compiler_params=pltpu.CompilerParams(
            collective_id=0, has_side_effects=True, vmem_limit_bytes=56 * 1024 * 1024
        ),
        name="arnoldi",
    )(
        jnp.transpose(basis, (0, 2, 1, 3)).reshape(KRYLOV * rows, 128),
        jnp.transpose(mie_coeffs, (1, 0, 2)),
        jnp.transpose(rot_table, (1, 0, 2)),
        jnp.transpose(axial_table, (0, 2, 1, 3)),
        jnp.transpose(pair_table, (2, 0, 1)),
        pair_count,
    )
    def direct(vector, norm_square):
        return lax.psum(jnp.sum(vector * vector), ("blk", "pair")) * MEAN_SCALE

    norm_square = lax.cond(flag[0] != 0, direct, lambda vector, norm_square: norm_square, vector, norm_square[0])
    vector = vector * lax.rsqrt(norm_square)
    return dots * MEAN_SCALE, jnp.transpose(vector.reshape(MODES, 2, 128), (1, 0, 2))


def solution(mesh):
    placed = (
        P(None, ("blk", "pair"), None, None),
        P(("blk", "pair"), None, None),
        P(),
        P(),
        P("blk", None, None),
        P("blk"),
    )
    return jax.shard_map(
        shards,
        mesh=mesh,
        in_specs=placed,
        out_specs=(P(), P(("blk", "pair"), None, None)),
        check_vma=False,
    )
```

```python
import functools

import jax
import jax.numpy as jnp
from jax import lax
from jax.experimental import pallas as pl
from jax.experimental.pallas import tpu as pltpu
from jax.sharding import PartitionSpec as P

MESH = pl.DeviceIdType.MESH
F32 = jnp.float32
BF16 = jnp.bfloat16
MODES = 510
PAD = 512
KRYLOV = 8
TABLES = 8
BLOCKS = 256
SPHERES = 64
ROWS = 16
CHUNKS = 2
LEAST = 0.01
MOST = 1e37
MEAN_SCALE = 1.0 / (BLOCKS * MODES * 2 * SPHERES)

NT = (((1,), (1,)), ((), ()))
NN = (((1,), (0,)), ((), ()))


def dot(left, right, dims):
    return lax.dot_general(left, right, dims, preferred_element_type=F32)


def times_i(value):
    lane = lax.broadcasted_iota(jnp.int32, value.shape, 1)
    turned = pltpu.roll(value, SPHERES, axis=1)
    return jnp.where(lane < SPHERES, -turned, turned)


def fold(value):
    rows = value.shape[0]
    whole = rows // 8 * 8
    total = value[:8]
    for start in range(8, whole, 8):
        total = total + value[start : start + 8]
    if rows > whole:
        rest = value[whole:]
        total = total + jnp.concatenate([rest, jnp.zeros((8 - rest.shape[0], 128), F32)], axis=0)
    return total


def row_pieces(step, total):
    return [(start, min(step, total - start)) for start in range(0, total, step)]


def count_matrix(pairs, member):
    row = lax.broadcasted_iota(jnp.int32, (256, 128), 0)
    g_row = (row >> 5).astype(F32)
    back = ((row >> 4) & 1) == 1
    own = (2 * member + ((row >> 3) & 1)).astype(F32)
    column = (lax.broadcasted_iota(jnp.int32, (192, 128), 0) >> 3).astype(F32)
    total = None
    for off, back_here in ((1, False), (0, True), (1, True), (2, True)):
        a, b, g = (pairs[off, n : n + 1, :] for n in range(3))
        right_table = jnp.where(g_row == g, 1.0, 0.0)
        if back_here:
            hit = jnp.where(back & (own + 8.0 * (2 - off) == b), right_table, 0.0)
            place = jnp.where(column == a + 8.0 * off, 1.0, 0.0)
        else:
            hit = jnp.where((~back) & (own == a), right_table, 0.0)
            place = jnp.where(column == b, 1.0, 0.0)
        term = dot(hit.astype(BF16), place.astype(BF16), NT)
        total = term if total is None else total + term
    same = (lax.broadcasted_iota(jnp.int32, (256, 192), 0) & 7) == (
        lax.broadcasted_iota(jnp.int32, (256, 192), 1) & 7
    )
    return jnp.where(same, total, 0.0).astype(BF16)


def aggregate(counts, win, sums, group):
    halves = []
    for slab in (2 * group, 2 * group + 1):
        part = win[:, slab].reshape(12 * ROWS, PAD)
        halves.append(dot(counts, part, NN).reshape(32, 8, PAD))
    sums[group] = jnp.concatenate(halves, axis=1).astype(BF16)


def field_of(sums, operators, field):
    groups = [[half * 4 + imag * 2 + n for half in range(2) for n in range(2)] for imag in range(2)]

    def gathered(g, direction):
        parts = []
        for imag in range(2):
            for t in range(2):
                parts.extend(sums[n, g * 4 + direction * 2 + t] for n in groups[imag])
        value = jnp.concatenate(parts, axis=0)
        return value, jnp.concatenate([-value[128:], value[:128]], axis=0)

    total = None
    for g in range(TABLES):
        for direction, dims in ((0, NT), (1, NN)):
            for part, value in enumerate(gathered(g, direction)):
                term = dot(value, operators[g, part], dims)
                total = term if total is None else total + term
    for imag in range(2):
        for t in range(2):
            start = (imag * 2 + t) * 64
            field[t, imag * 64 : imag * 64 + 64] = total[start : start + 64]


def kernel(
    basis_hbm, mie_hbm, rot_hbm, axial_hbm, table_hbm, count_ref,
    proj_ref, out_ref, norm_ref, flag_ref,
    basis, mie_raw, mie, rot_raw, axial_raw, rot, axial, operators, table, current, pairs, win, sums, field, mixed, image, red_a, red_b,
    load_sem, send_sem, recv_sem, pair_send, pair_recv, a_send, a_recv, b_send, b_recv, share_send, share_recv, far_sem,
):
    blk_ways, pair_ways = lax.axis_size("blk"), lax.axis_size("pair")
    blk, member = lax.axis_index("blk"), lax.axis_index("pair")
    core = lax.rem(blk, 2)
    row = blk // 2
    row_ways = blk_ways // 2
    inner = blk + 1 - 2 * core
    outer = lax.rem(blk - 1 + 2 * core + blk_ways, blk_ways)
    right, left, far = (lax.rem(member + n, pair_ways) for n in (1, 3, 2))

    last = KRYLOV - 1
    rows = 2 * MODES
    share = TABLES // 2
    first_rows = last * rows // 8 * 8
    head, tail = pl.ds(0, first_rows), pl.ds(first_rows, KRYLOV * rows - first_rows)
    load_last = pltpu.make_async_copy(basis_hbm.at[tail], basis.at[tail], load_sem.at[0])
    load_table = pltpu.make_async_copy(table_hbm, table, load_sem.at[1])
    load_rot = pltpu.make_async_copy(rot_hbm, rot_raw, load_sem.at[2])
    load_axial = [
        pltpu.make_async_copy(axial_hbm.at[core * share + n], axial_raw.at[n], load_sem.at[5 + n])
        for n in range(share)
    ]
    load_rest = pltpu.make_async_copy(basis_hbm.at[head], basis.at[head], load_sem.at[3])
    load_mie = pltpu.make_async_copy(mie_hbm, mie_raw, load_sem.at[4])
    for load in [load_last, load_table, load_rot, *load_axial, load_rest, load_mie]:
        load.start()

    spot = core * pair_ways + member
    group_a = []
    for n in (2, 6, 1, 3, 5, 7, 4):
        other = lax.rem(spot + n, 2 * pair_ways)
        group_a.append((other, (2 * row + other // pair_ways, lax.rem(other, pair_ways))))
    group_b = []
    high, low = row // 4, lax.rem(row, 4)
    steps = [(n, m) for n in range(4) for m in range(4) if n or m]
    for n, m in sorted(steps, key=lambda step: -min(step[0], 4 - step[0]) - min(step[1], 4 - step[1])):
        other = 4 * lax.rem(high + n, 4) + lax.rem(low + m, 4)
        group_b.append((other, (2 * other + core, member)))
    barrier = pltpu.get_barrier_semaphore()
    beside_low = [(2 * (4 * high + lax.rem(low + n, 4)) + core, member) for n in (1, 3)]
    beside_high = [(2 * (4 * lax.rem(high + n, 4) + low) + core, member) for n in (1, 3)]
    near = [(outer, member)] + [d for _, d in group_a] + beside_low + beside_high
    for device in near:
        pl.semaphore_signal(barrier, inc=1, device_id=device, device_id_type=MESH)

    def pass_on(turn):
        for device in beside_high if turn else beside_low:
            pl.semaphore_signal(far_sem.at[turn], inc=1, device_id=device, device_id_type=MESH)

    load_last.wait()
    current[:, pl.ds(MODES - 6, 8), :] = jnp.zeros((2, 8, 128), F32)
    mine = 4 + member
    for t in range(2):
        current[t, pl.ds(0, MODES), :] = basis[pl.ds(last * rows + t, MODES, stride=2), :]
    flipped = [jnp.transpose(current[t]) for t in range(2)]
    for slab in range(16):
        half, imag, q = slab // 8, slab // 4 % 2, slab % 4
        start = imag * 64 + half * 32 + q * 8
        both = jnp.concatenate([value[start : start + 8] for value in flipped], axis=0)
        win[mine, slab] = both.astype(BF16)
    pl.semaphore_wait(barrier, len(near))

    width = 16 // CHUNKS
    sends = []
    window_sends = list(range(11 * CHUNKS))

    def send(source_slot, target_slot, chunk, device):
        place = pl.ds(chunk * width, width)
        copy = pltpu.make_async_remote_copy(
            src_ref=win.at[source_slot, place],
            dst_ref=win.at[target_slot, place],
            send_sem=send_sem.at[window_sends.pop()],
            recv_sem=recv_sem.at[target_slot * CHUNKS + chunk],
            device_id=device,
            device_id_type=MESH,
        )
        copy.start()
        sends.append(copy)

    def arrived(slot, chunk):
        place = pl.ds(chunk * width, width)
        pltpu.make_async_remote_copy(
            src_ref=win.at[slot, place],
            dst_ref=win.at[slot, place],
            send_sem=send_sem.at[0],
            recv_sem=recv_sem.at[slot * CHUNKS + chunk],
            device_id=(inner, member),
            device_id_type=MESH,
        ).wait_recv()

    to_inner, to_outer = 8 * core, 8 * (1 - core)
    from_inner, from_outer = 8 * (1 - core), 8 * core
    for chunk in range(CHUNKS):
        send(mine, to_outer + member, chunk, (outer, member))
        send(mine, mine, chunk, (blk, right))
        send(mine, mine, chunk, (blk, left))
        send(mine, to_inner + member, chunk, (inner, member))

    load_table.wait()
    live = lax.broadcasted_iota(jnp.int32, (1, 128), 1) < count_ref[0]
    pairs[1, pl.ds(0, 1), :] = table[0].astype(F32)
    pairs[1, pl.ds(1, 1), :] = table[1].astype(F32)
    pairs[1, pl.ds(2, 1), :] = jnp.where(live, table[2].astype(F32), -1.0)
    pairs[1, pl.ds(3, 5), :] = jnp.zeros((5, 128), F32)
    pair_copies = []
    for n, (slot, device) in enumerate(((2 * core, (inner, member)), (2 - 2 * core, (outer, member)))):
        copy = pltpu.make_async_remote_copy(
            src_ref=pairs.at[1],
            dst_ref=pairs.at[slot],
            send_sem=pair_send.at[n],
            recv_sem=pair_recv.at[n],
            device_id=device,
            device_id_type=MESH,
        )
        copy.start()
        pair_copies.append(copy)

    def forward(chunk):
        for origin, keep_on, device in ((left, 0, right), (right, 1, left)):
            arrived(4 + origin, chunk)
            send(4 + origin, to_outer + origin, chunk, (outer, member))
            if chunk % 2 == keep_on:
                send(4 + origin, 4 + origin, chunk, (blk, device))
            send(4 + origin, to_inner + origin, chunk, (inner, member))

    def forward_far(chunk):
        arrived(4 + far, chunk)
        send(4 + far, to_outer + far, chunk, (outer, member))
        send(4 + far, to_inner + far, chunk, (inner, member))

    def landed(chunks):
        for chunk in chunks:
            for n in range(pair_ways):
                arrived(from_inner + n, chunk)
                arrived(from_outer + n, chunk)

    rot[:, pl.ds(PAD - 16, 16), :] = jnp.zeros((TABLES, 16, PAD), BF16)
    rot[:, :, pl.ds(PAD - 128, 128)] = jnp.zeros((TABLES, PAD, 128), BF16)

    def order_rot():
        load_rot.wait()
        for start, size in row_pieces(32, MODES):
            value = rot_raw[pl.ds(start, size)]
            rot[:, pl.ds(start, size), pl.ds(0, MODES)] = jnp.swapaxes(value, 0, 1)

    def order_axial(g):
        for start, size in row_pieces(64, MODES):
            value = axial_raw[g, pl.ds(start, size)]
            axial[g % 2, :, pl.ds(start, size), pl.ds(0, MODES)] = jnp.swapaxes(value, 0, 1)

    def shared(n, first):
        place = operators.at[first + n]
        return pltpu.make_async_remote_copy(
            src_ref=place,
            dst_ref=place,
            send_sem=share_send.at[n],
            recv_sem=share_recv.at[n],
            device_id=(inner, member),
            device_id_type=MESH,
        )

    def operator(n):
        g = core * share + n
        rotation = rot[g]
        flipped = jnp.transpose(rotation)
        for part in range(2):
            moved = dot(axial[n % 2, part], rotation, NN).astype(BF16)
            operators[g, part] = dot(flipped, moved, NN).astype(BF16)
        copy = shared(n, core * share)
        copy.start()
        sends.append(copy)

    lines = []

    def gram_line(j):
        lane = lax.broadcasted_iota(jnp.int32, (1, 128), 1)
        real = [jnp.zeros((8, 128), F32)] * KRYLOV
        imag = [jnp.zeros((8, 128), F32)] * KRYLOV
        for start, size in row_pieces(64, rows):
            one = basis[pl.ds(j * rows + start, size), :]
            turned = times_i(one)
            for k in range(j, KRYLOV):
                other = basis[pl.ds(k * rows + start, size), :]
                real[k] = real[k] + fold(one * other)
                if k > j:
                    imag[k] = imag[k] + fold(turned * other)
        line = jnp.zeros((1, 128), F32)
        for k in range(j, KRYLOV):
            line = jnp.where(lane == 8 + k, jnp.sum(real[k]), line)
            if k > j:
                line = jnp.where(lane == 16 + k, jnp.sum(imag[k]), line)
        lines.append(line)

    def order_mie():
        for start, size in row_pieces(32, MODES):
            scale = mie_raw[pl.ds(start, size)].reshape(2 * size, 128)
            lane = lax.broadcasted_iota(jnp.int32, scale.shape, 1)
            other = pltpu.roll(scale, SPHERES, axis=1)
            mie[0, pl.ds(2 * start, 2 * size), :] = jnp.where(lane < SPHERES, scale, other)
            mie[1, pl.ds(2 * start, 2 * size), :] = jnp.where(lane < SPHERES, other, scale)

    axial[:, :, pl.ds(PAD - 16, 16), :] = jnp.zeros((2, 2, 16, PAD), BF16)
    axial[:, :, :, pl.ds(PAD - 128, 128)] = jnp.zeros((2, 2, PAD, 128), BF16)
    pass_on(0)
    order_rot()
    load_axial[0].wait()
    order_axial(0)
    load_axial[1].wait()
    order_axial(1)
    operator(0)
    forward(0)
    load_axial[2].wait()
    load_rest.wait()
    order_axial(2)
    operator(1)
    gram_line(0)
    pl.semaphore_wait(far_sem.at[0], 2)
    pass_on(1)
    forward(1)
    load_axial[3].wait()
    order_axial(3)
    operator(2)
    gram_line(1)
    forward_far(0)
    pl.semaphore_wait(far_sem.at[1], 2)
    pass_on(2)
    operator(3)
    gram_line(2)
    forward_far(1)
    load_mie.wait()
    for copy in pair_copies:
        copy.wait()
    for j in range(3, KRYLOV):
        gram_line(j)
    packed_gram = jnp.concatenate(lines, axis=0)
    counts = count_matrix(pairs, member)
    order_mie()
    pl.semaphore_wait(far_sem.at[2], 2)
    for n in range(share):
        shared(n, (1 - core) * share).wait_recv()
    landed(range(CHUNKS))
    for group in range(8):
        aggregate(counts, win, sums, group)
    field_of(sums, operators, field)

    real = [jnp.zeros((8, 128), F32)] * KRYLOV
    imag = [jnp.zeros((8, 128), F32)] * KRYLOV
    square = jnp.zeros((8, 128), F32)
    for t in range(2):
        mixed[pl.ds(t, PAD, stride=2), :] = jnp.transpose(field[t])
    for start, size in row_pieces(64, rows):
        place = pl.ds(start, size)
        here = mixed[place, :]
        product = mie[0, place, :] * here + mie[1, place, :] * times_i(here)
        value = basis[pl.ds(last * rows + start, size), :] - product
        image[place, :] = value
        turned = times_i(value)
        square = square + fold(value * value)
        for k in range(KRYLOV):
            vector = basis[pl.ds(k * rows + start, size), :]
            real[k] = real[k] + fold(vector * value)
            imag[k] = imag[k] - fold(vector * turned)

    def tile_of(parts):
        rows = [jnp.sum(part, axis=0, keepdims=True) for part in parts]
        return jnp.sum(jnp.concatenate(rows, axis=0), axis=1, keepdims=True)

    def all_sum(call, value):
        steps = ((red_a, a_send, a_recv, group_a, spot), (red_b, b_send, b_recv, group_b, row))
        for store, send_sems, recv_sems, group, index in steps:
            store[call, index] = value
            copies = []
            for n, (other, device) in enumerate(group):
                copy = pltpu.make_async_remote_copy(
                    src_ref=store.at[call, index],
                    dst_ref=store.at[call, index],
                    send_sem=send_sems.at[call, n],
                    recv_sem=recv_sems.at[call, index],
                    device_id=device,
                    device_id_type=MESH,
                )
                copy.start()
                copies.append(copy)
            for copy in sends:
                copy.wait_send()
            sends.clear()
            for other, device in group:
                pltpu.make_async_remote_copy(
                    src_ref=store.at[call, other],
                    dst_ref=store.at[call, other],
                    send_sem=send_sems.at[call, 0],
                    recv_sem=recv_sems.at[call, other],
                    device_id=device,
                    device_id_type=MESH,
                ).wait_recv()
            value = store[call, 0]
            for n in range(1, len(group) + 1):
                value = value + store[call, n]
            sends.extend(copies)
        return value

    lane = lax.broadcasted_iota(jnp.int32, (8, 128), 1)
    packed = jnp.where(lane == 0, tile_of(real), jnp.where(lane == 1, tile_of(imag), packed_gram))
    packed = jnp.where(lane == 2, jnp.sum(square) * 0.125, packed)
    reduced = all_sum(0, packed)
    dots = reduced * MEAN_SCALE
    turned_dots = jnp.transpose(jnp.concatenate([dots, jnp.zeros((120, 128), F32)], axis=0))
    proj_ref[...] = jnp.transpose(jnp.concatenate([reduced, jnp.zeros((120, 128), F32)], axis=0))[:2, :KRYLOV]

    first, second = jnp.where(lane < KRYLOV, turned_dots[0:1], 0.0), jnp.where(lane < KRYLOV, turned_dots[1:2], 0.0)
    c_real, c_imag = dots[:, 0:1], dots[:, 1:2]
    weight = jnp.where(lane == lax.broadcasted_iota(jnp.int32, (8, 128), 0), 1.0, 2.0)
    gram_real, gram_imag = pltpu.roll(reduced, 120, axis=1), pltpu.roll(reduced, 112, axis=1)
    form = (c_real * first + c_imag * second) * gram_real - (c_real * second - c_imag * first) * gram_imag
    quadratic = jnp.sum(jnp.where(lane < KRYLOV, weight * form, 0.0)) * MEAN_SCALE
    linear = 2.0 * jnp.sum(jnp.where(lane < 2, dots * dots, 0.0))
    constant = jnp.sum(jnp.where(lane == 2, dots, 0.0))
    norm_square = constant - linear + quadratic
    fine = (norm_square > LEAST * (constant + linear + quadratic)) & (norm_square < MOST)
    norm_ref[0] = norm_square
    flag_ref[0] = jnp.where(fine, 0, 1)

    for start, size in row_pieces(64, rows):
        place = pl.ds(start, size)
        plain = image[place, :]
        turned = jnp.zeros((size, 128), F32)
        for k in range(KRYLOV):
            vector = basis[pl.ds(k * rows + start, size), :]
            plain = plain - dots[k : k + 1, 0:1] * vector
            turned = turned + dots[k : k + 1, 1:2] * vector
        out_ref[place, :] = plain - times_i(turned)
    for copy in sends:
        copy.wait_send()


def shards(basis, mie_coeffs, rot_table, axial_table, pair_table, pair_count):
    rows = 2 * MODES
    anywhere = pl.BlockSpec(memory_space=pl.ANY)
    dots, vector, norm_square, flag = pl.pallas_call(
        kernel,
        out_shape=(
            jax.ShapeDtypeStruct((2, KRYLOV), F32),
            jax.ShapeDtypeStruct((rows, 2 * SPHERES), F32),
            jax.ShapeDtypeStruct((1,), F32),
            jax.ShapeDtypeStruct((1,), jnp.int32),
        ),
        in_specs=[anywhere] * 5 + [pl.BlockSpec(memory_space=pltpu.SMEM)],
        out_specs=(pl.BlockSpec(memory_space=pltpu.VMEM),) * 2 + (pl.BlockSpec(memory_space=pltpu.SMEM),) * 2,
        scratch_shapes=[
            pltpu.VMEM((KRYLOV * rows, 128), F32),
            pltpu.VMEM((MODES, 2, 128), F32),
            pltpu.VMEM((2, rows, 128), F32),
            pltpu.VMEM((MODES, TABLES, MODES), BF16),
            pltpu.VMEM((TABLES // 2, MODES, 2, MODES), BF16),
            pltpu.VMEM((TABLES, PAD, PAD), BF16),
            pltpu.VMEM((2, 2, PAD, PAD), BF16),
            pltpu.VMEM((TABLES, 2, PAD, PAD), BF16),
            pltpu.VMEM((3, 1, 128), jnp.int32),
            pltpu.VMEM((2, PAD, 128), F32),
            pltpu.VMEM((3, 8, 128), F32),
            pltpu.VMEM((12, 16, ROWS, PAD), BF16),
            pltpu.VMEM((8, 32, ROWS, PAD), BF16),
            pltpu.VMEM((2, 128, PAD), F32),
            pltpu.VMEM((2 * PAD, 128), F32),
            pltpu.VMEM((rows, 128), F32),
            pltpu.VMEM((1, 8, 8, 128), F32),
            pltpu.VMEM((1, 16, 8, 128), F32),
            pltpu.SemaphoreType.DMA((13,)),
            pltpu.SemaphoreType.DMA((11 * CHUNKS,)),
            pltpu.SemaphoreType.DMA((12 * CHUNKS,)),
            pltpu.SemaphoreType.DMA((2,)),
            pltpu.SemaphoreType.DMA((2,)),
            pltpu.SemaphoreType.DMA((1, 7)),
            pltpu.SemaphoreType.DMA((1, 8)),
            pltpu.SemaphoreType.DMA((1, 15)),
            pltpu.SemaphoreType.DMA((1, 16)),
            pltpu.SemaphoreType.DMA((TABLES // 2,)),
            pltpu.SemaphoreType.DMA((TABLES // 2,)),
            pltpu.SemaphoreType.REGULAR((3,)),
        ],
        compiler_params=pltpu.CompilerParams(
            collective_id=0, has_side_effects=True, vmem_limit_bytes=56 * 1024 * 1024
        ),
        name="arnoldi",
    )(
        jnp.transpose(basis, (0, 2, 1, 3)).reshape(KRYLOV * rows, 128),
        jnp.transpose(mie_coeffs, (1, 0, 2)),
        jnp.transpose(rot_table, (1, 0, 2)),
        jnp.transpose(axial_table, (0, 2, 1, 3)),
        jnp.transpose(pair_table, (2, 0, 1)),
        pair_count,
    )
    def direct(vector, norm_square):
        return lax.psum(jnp.sum(vector * vector), ("blk", "pair")) * MEAN_SCALE

    norm_square = lax.cond(flag[0] != 0, direct, lambda vector, norm_square: norm_square, vector, norm_square[0])
    vector = vector * lax.rsqrt(norm_square)
    return dots * MEAN_SCALE, jnp.transpose(vector.reshape(MODES, 2, 128), (1, 0, 2))


def solution(mesh):
    placed = (
        P(None, ("blk", "pair"), None, None),
        P(("blk", "pair"), None, None),
        P(),
        P(),
        P("blk", None, None),
        P("blk"),
    )
    return jax.shard_map(
        shards,
        mesh=mesh,
        in_specs=placed,
        out_specs=(P(), P(("blk", "pair"), None, None)),
        check_vma=False,
    )
```

```python
import functools

import jax
import jax.numpy as jnp
from jax import lax
from jax.experimental import pallas as pl
from jax.experimental.pallas import tpu as pltpu
from jax.sharding import PartitionSpec as P

MESH = pl.DeviceIdType.MESH
F32 = jnp.float32
BF16 = jnp.bfloat16
MODES = 510
PAD = 512
KRYLOV = 8
TABLES = 8
BLOCKS = 256
SPHERES = 64
ROWS = 16
CHUNKS = 2
LEAST = 0.01
MOST = 1e37
MEAN_SCALE = 1.0 / (BLOCKS * MODES * 2 * SPHERES)

NT = (((1,), (1,)), ((), ()))
NN = (((1,), (0,)), ((), ()))


def dot(left, right, dims):
    return lax.dot_general(left, right, dims, preferred_element_type=F32)


def times_i(value):
    lane = lax.broadcasted_iota(jnp.int32, value.shape, 1)
    turned = pltpu.roll(value, SPHERES, axis=1)
    return jnp.where(lane < SPHERES, -turned, turned)


def fold(value):
    rows = value.shape[0]
    whole = rows // 8 * 8
    total = value[:8]
    for start in range(8, whole, 8):
        total = total + value[start : start + 8]
    if rows > whole:
        rest = value[whole:]
        total = total + jnp.concatenate([rest, jnp.zeros((8 - rest.shape[0], 128), F32)], axis=0)
    return total


def row_pieces(step, total):
    return [(start, min(step, total - start)) for start in range(0, total, step)]


def count_matrix(pairs, member):
    row = lax.broadcasted_iota(jnp.int32, (256, 128), 0)
    g_row = (row >> 5).astype(F32)
    back = ((row >> 4) & 1) == 1
    own = (2 * member + ((row >> 3) & 1)).astype(F32)
    column = (lax.broadcasted_iota(jnp.int32, (192, 128), 0) >> 3).astype(F32)
    total = None
    for off, back_here in ((1, False), (0, True), (1, True), (2, True)):
        a, b, g = (pairs[off, n : n + 1, :] for n in range(3))
        right_table = jnp.where(g_row == g, 1.0, 0.0)
        if back_here:
            hit = jnp.where(back & (own + 8.0 * (2 - off) == b), right_table, 0.0)
            place = jnp.where(column == a + 8.0 * off, 1.0, 0.0)
        else:
            hit = jnp.where((~back) & (own == a), right_table, 0.0)
            place = jnp.where(column == b, 1.0, 0.0)
        term = dot(hit.astype(BF16), place.astype(BF16), NT)
        total = term if total is None else total + term
    same = (lax.broadcasted_iota(jnp.int32, (256, 192), 0) & 7) == (
        lax.broadcasted_iota(jnp.int32, (256, 192), 1) & 7
    )
    return jnp.where(same, total, 0.0).astype(BF16)


def aggregate(counts, win, sums, group):
    halves = []
    for slab in (2 * group, 2 * group + 1):
        part = win[:, slab].reshape(12 * ROWS, PAD)
        halves.append(dot(counts, part, NN).reshape(32, 8, PAD))
    sums[group] = jnp.concatenate(halves, axis=1).astype(BF16)


def field_of(sums, operators, field):
    groups = [[half * 4 + imag * 2 + n for half in range(2) for n in range(2)] for imag in range(2)]

    def gathered(g, direction):
        parts = []
        for imag in range(2):
            for t in range(2):
                parts.extend(sums[n, g * 4 + direction * 2 + t] for n in groups[imag])
        value = jnp.concatenate(parts, axis=0)
        return value, jnp.concatenate([-value[128:], value[:128]], axis=0)

    total = None
    for g in range(TABLES):
        for direction, dims in ((0, NT), (1, NN)):
            for part, value in enumerate(gathered(g, direction)):
                term = dot(value, operators[g, part], dims)
                total = term if total is None else total + term
    for imag in range(2):
        for t in range(2):
            start = (imag * 2 + t) * 64
            field[t, imag * 64 : imag * 64 + 64] = total[start : start + 64]


def kernel(
    basis_hbm, mie_hbm, rot_hbm, axial_hbm, table_hbm, count_ref,
    proj_ref, out_ref, norm_ref, flag_ref,
    basis, mie_raw, mie, rot_raw, axial_raw, rot, axial, operators, table, current, pairs, win, sums, field, mixed, image, red_a, red_b,
    load_sem, send_sem, recv_sem, pair_send, pair_recv, a_send, a_recv, b_send, b_recv, share_send, share_recv, far_sem,
):
    blk_ways, pair_ways = lax.axis_size("blk"), lax.axis_size("pair")
    blk, member = lax.axis_index("blk"), lax.axis_index("pair")
    core = lax.rem(blk, 2)
    row = blk // 2
    row_ways = blk_ways // 2
    inner = blk + 1 - 2 * core
    outer = lax.rem(blk - 1 + 2 * core + blk_ways, blk_ways)
    right, left, far = (lax.rem(member + n, pair_ways) for n in (1, 3, 2))

    last = KRYLOV - 1
    rows = 2 * MODES
    share = TABLES // 2
    first_rows = last * rows // 8 * 8
    head, tail = pl.ds(0, first_rows), pl.ds(first_rows, KRYLOV * rows - first_rows)
    load_last = pltpu.make_async_copy(basis_hbm.at[tail], basis.at[tail], load_sem.at[0])
    load_table = pltpu.make_async_copy(table_hbm, table, load_sem.at[1])
    load_rot = pltpu.make_async_copy(rot_hbm, rot_raw, load_sem.at[2])
    load_axial = [
        pltpu.make_async_copy(axial_hbm.at[core * share + n], axial_raw.at[n], load_sem.at[5 + n])
        for n in range(share)
    ]
    load_rest = pltpu.make_async_copy(basis_hbm.at[head], basis.at[head], load_sem.at[3])
    load_mie = pltpu.make_async_copy(mie_hbm, mie_raw, load_sem.at[4])
    for load in [load_last, load_table, load_rot, *load_axial, load_rest, load_mie]:
        load.start()

    spot = core * pair_ways + member
    group_a = []
    for n in (2, 6, 1, 3, 5, 7, 4):
        other = lax.rem(spot + n, 2 * pair_ways)
        group_a.append((other, (2 * row + other // pair_ways, lax.rem(other, pair_ways))))
    group_b = []
    high, low = row // 4, lax.rem(row, 4)
    steps = [(n, m) for n in range(4) for m in range(4) if n or m]
    for n, m in sorted(steps, key=lambda step: -min(step[0], 4 - step[0]) - min(step[1], 4 - step[1])):
        other = 4 * lax.rem(high + n, 4) + lax.rem(low + m, 4)
        group_b.append((other, (2 * other + core, member)))
    barrier = pltpu.get_barrier_semaphore()
    def beside(distance):
        steps = (distance, row_ways - distance)
        return [(2 * lax.rem(row + n, row_ways) + core, member) for n in steps]

    near = [(outer, member), (blk, right), (blk, left), (inner, member)]
    rounds = [near, [(inner, member)] + beside(1), beside(2), beside(4)]
    for device in near:
        pl.semaphore_signal(barrier, inc=1, device_id=device, device_id_type=MESH)

    def pass_on(turn):
        if turn:
            pl.semaphore_wait(far_sem.at[turn - 1], len(rounds[turn - 1]))
        for device in rounds[turn]:
            pl.semaphore_signal(far_sem.at[turn], inc=1, device_id=device, device_id_type=MESH)

    load_last.wait()
    current[:, pl.ds(MODES - 6, 8), :] = jnp.zeros((2, 8, 128), F32)
    mine = 4 + member
    for t in range(2):
        current[t, pl.ds(0, MODES), :] = basis[pl.ds(last * rows + t, MODES, stride=2), :]
    flipped = [jnp.transpose(current[t]) for t in range(2)]

    def place(half):
        for slab in range(8 * half, 8 * half + 8):
            start = slab // 4 % 2 * 64 + half * 32 + slab % 4 * 8
            both = jnp.concatenate([value[start : start + 8] for value in flipped], axis=0)
            win[mine, slab] = both.astype(BF16)

    place(0)
    place(1)
    pl.semaphore_wait(barrier, len(near))

    width = 16 // CHUNKS
    sends = []
    window_sends = list(range(11 * CHUNKS))

    def send(source_slot, target_slot, chunk, device):
        span = pl.ds(chunk * width, width)
        copy = pltpu.make_async_remote_copy(
            src_ref=win.at[source_slot, span],
            dst_ref=win.at[target_slot, span],
            send_sem=send_sem.at[window_sends.pop()],
            recv_sem=recv_sem.at[target_slot * CHUNKS + chunk],
            device_id=device,
            device_id_type=MESH,
        )
        copy.start()
        sends.append(copy)

    def arrived(slot, chunk):
        span = pl.ds(chunk * width, width)
        pltpu.make_async_remote_copy(
            src_ref=win.at[slot, span],
            dst_ref=win.at[slot, span],
            send_sem=send_sem.at[0],
            recv_sem=recv_sem.at[slot * CHUNKS + chunk],
            device_id=(inner, member),
            device_id_type=MESH,
        ).wait_recv()

    to_inner, to_outer = 8 * core, 8 * (1 - core)
    from_inner, from_outer = 8 * (1 - core), 8 * core
    for chunk in range(CHUNKS):
        send(mine, to_outer + member, chunk, (outer, member))
        send(mine, mine, chunk, (blk, right))
        send(mine, mine, chunk, (blk, left))
        send(mine, to_inner + member, chunk, (inner, member))

    load_table.wait()
    live = lax.broadcasted_iota(jnp.int32, (1, 128), 1) < count_ref[0]
    pairs[1, pl.ds(0, 1), :] = table[0].astype(F32)
    pairs[1, pl.ds(1, 1), :] = table[1].astype(F32)
    pairs[1, pl.ds(2, 1), :] = jnp.where(live, table[2].astype(F32), -1.0)
    pairs[1, pl.ds(3, 5), :] = jnp.zeros((5, 128), F32)
    pair_copies = []
    for n, (slot, device) in enumerate(((2 * core, (inner, member)), (2 - 2 * core, (outer, member)))):
        copy = pltpu.make_async_remote_copy(
            src_ref=pairs.at[1],
            dst_ref=pairs.at[slot],
            send_sem=pair_send.at[n],
            recv_sem=pair_recv.at[n],
            device_id=device,
            device_id_type=MESH,
        )
        copy.start()
        pair_copies.append(copy)

    def forward(chunk):
        for origin, keep_on, device in ((left, 0, right), (right, 1, left)):
            arrived(4 + origin, chunk)
            if chunk % 2 == keep_on:
                send(4 + origin, 4 + origin, chunk, (blk, device))
            send(4 + origin, to_outer + origin, chunk, (outer, member))
            send(4 + origin, to_inner + origin, chunk, (inner, member))

    def forward_far(chunk):
        arrived(4 + far, chunk)
        send(4 + far, to_outer + far, chunk, (outer, member))
        send(4 + far, to_inner + far, chunk, (inner, member))

    def landed(chunks):
        for chunk in chunks:
            for n in range(pair_ways):
                arrived(from_inner + n, chunk)
                arrived(from_outer + n, chunk)

    rot[:, pl.ds(PAD - 16, 16), :] = jnp.zeros((TABLES, 16, PAD), BF16)
    rot[:, :, pl.ds(PAD - 128, 128)] = jnp.zeros((TABLES, PAD, 128), BF16)

    def order_rot():
        load_rot.wait()
        for start, size in row_pieces(32, MODES):
            value = rot_raw[pl.ds(start, size)]
            rot[:, pl.ds(start, size), pl.ds(0, MODES)] = jnp.swapaxes(value, 0, 1)

    def order_axial(g):
        for start, size in row_pieces(64, MODES):
            value = axial_raw[g, pl.ds(start, size)]
            axial[g % 2, :, pl.ds(start, size), pl.ds(0, MODES)] = jnp.swapaxes(value, 0, 1)

    def shared(n, first):
        place = operators.at[first + n]
        return pltpu.make_async_remote_copy(
            src_ref=place,
            dst_ref=place,
            send_sem=share_send.at[n],
            recv_sem=share_recv.at[n],
            device_id=(inner, member),
            device_id_type=MESH,
        )

    def operator(n):
        g = core * share + n
        rotation = rot[g]
        flipped = jnp.transpose(rotation)
        for part in range(2):
            moved = dot(axial[n % 2, part], rotation, NN).astype(BF16)
            operators[g, part] = dot(flipped, moved, NN).astype(BF16)
        copy = shared(n, core * share)
        copy.start()
        sends.append(copy)

    lines = []

    def gram_line(j):
        lane = lax.broadcasted_iota(jnp.int32, (1, 128), 1)
        real = [jnp.zeros((8, 128), F32)] * KRYLOV
        imag = [jnp.zeros((8, 128), F32)] * KRYLOV
        for start, size in row_pieces(64, rows):
            one = basis[pl.ds(j * rows + start, size), :]
            turned = times_i(one)
            for k in range(j, KRYLOV):
                other = basis[pl.ds(k * rows + start, size), :]
                real[k] = real[k] + fold(one * other)
                if k > j:
                    imag[k] = imag[k] + fold(turned * other)
        line = jnp.zeros((1, 128), F32)
        for k in range(j, KRYLOV):
            line = jnp.where(lane == 8 + k, jnp.sum(real[k]), line)
            if k > j:
                line = jnp.where(lane == 16 + k, jnp.sum(imag[k]), line)
        lines.append(line)

    def order_mie():
        for start, size in row_pieces(32, MODES):
            scale = mie_raw[pl.ds(start, size)].reshape(2 * size, 128)
            lane = lax.broadcasted_iota(jnp.int32, scale.shape, 1)
            other = pltpu.roll(scale, SPHERES, axis=1)
            mie[0, pl.ds(2 * start, 2 * size), :] = jnp.where(lane < SPHERES, scale, other)
            mie[1, pl.ds(2 * start, 2 * size), :] = jnp.where(lane < SPHERES, other, scale)

    axial[:, :, pl.ds(PAD - 16, 16), :] = jnp.zeros((2, 2, 16, PAD), BF16)
    axial[:, :, :, pl.ds(PAD - 128, 128)] = jnp.zeros((2, 2, PAD, 128), BF16)
    pass_on(0)
    order_rot()
    load_axial[0].wait()
    order_axial(0)
    load_axial[1].wait()
    order_axial(1)
    operator(0)
    forward(0)
    load_axial[2].wait()
    load_rest.wait()
    order_axial(2)
    operator(1)
    gram_line(0)
    pass_on(1)
    forward(1)
    load_axial[3].wait()
    order_axial(3)
    operator(2)
    operator(3)
    pass_on(2)
    forward_far(0)
    forward_far(1)
    pass_on(3)
    gram_line(1)
    gram_line(2)
    load_mie.wait()
    for copy in pair_copies:
        copy.wait()
    for j in range(3, KRYLOV):
        gram_line(j)
    packed_gram = jnp.concatenate(lines, axis=0)
    counts = count_matrix(pairs, member)
    order_mie()
    pl.semaphore_wait(far_sem.at[3], len(rounds[3]))
    for n in range(share):
        shared(n, (1 - core) * share).wait_recv()
    landed(range(CHUNKS))
    for group in range(8):
        aggregate(counts, win, sums, group)
    field_of(sums, operators, field)

    real = [jnp.zeros((8, 128), F32)] * KRYLOV
    imag = [jnp.zeros((8, 128), F32)] * KRYLOV
    square = jnp.zeros((8, 128), F32)
    for t in range(2):
        mixed[pl.ds(t, PAD, stride=2), :] = jnp.transpose(field[t])
    for start, size in row_pieces(64, rows):
        place = pl.ds(start, size)
        here = mixed[place, :]
        product = mie[0, place, :] * here + mie[1, place, :] * times_i(here)
        value = basis[pl.ds(last * rows + start, size), :] - product
        image[place, :] = value
        turned = times_i(value)
        square = square + fold(value * value)
        for k in range(KRYLOV):
            vector = basis[pl.ds(k * rows + start, size), :]
            real[k] = real[k] + fold(vector * value)
            imag[k] = imag[k] - fold(vector * turned)

    def tile_of(parts):
        rows = [jnp.sum(part, axis=0, keepdims=True) for part in parts]
        return jnp.sum(jnp.concatenate(rows, axis=0), axis=1, keepdims=True)

    def all_sum(call, value):
        steps = ((red_a, a_send, a_recv, group_a, spot), (red_b, b_send, b_recv, group_b, row))
        for store, send_sems, recv_sems, group, index in steps:
            store[call, index] = value
            copies = []
            for n, (other, device) in enumerate(group):
                copy = pltpu.make_async_remote_copy(
                    src_ref=store.at[call, index],
                    dst_ref=store.at[call, index],
                    send_sem=send_sems.at[call, n],
                    recv_sem=recv_sems.at[call, index],
                    device_id=device,
                    device_id_type=MESH,
                )
                copy.start()
                copies.append(copy)
            for copy in sends:
                copy.wait_send()
            sends.clear()
            for other, device in group:
                pltpu.make_async_remote_copy(
                    src_ref=store.at[call, other],
                    dst_ref=store.at[call, other],
                    send_sem=send_sems.at[call, 0],
                    recv_sem=recv_sems.at[call, other],
                    device_id=device,
                    device_id_type=MESH,
                ).wait_recv()
            value = store[call, 0]
            for n in range(1, len(group) + 1):
                value = value + store[call, n]
            sends.extend(copies)
        return value

    lane = lax.broadcasted_iota(jnp.int32, (8, 128), 1)
    packed = jnp.where(lane == 0, tile_of(real), jnp.where(lane == 1, tile_of(imag), packed_gram))
    packed = jnp.where(lane == 2, jnp.sum(square) * 0.125, packed)
    reduced = all_sum(0, packed)
    dots = reduced * MEAN_SCALE
    turned_dots = jnp.transpose(jnp.concatenate([dots, jnp.zeros((120, 128), F32)], axis=0))
    proj_ref[...] = jnp.transpose(jnp.concatenate([reduced, jnp.zeros((120, 128), F32)], axis=0))[:2, :KRYLOV]

    first, second = jnp.where(lane < KRYLOV, turned_dots[0:1], 0.0), jnp.where(lane < KRYLOV, turned_dots[1:2], 0.0)
    c_real, c_imag = dots[:, 0:1], dots[:, 1:2]
    weight = jnp.where(lane == lax.broadcasted_iota(jnp.int32, (8, 128), 0), 1.0, 2.0)
    gram_real, gram_imag = pltpu.roll(reduced, 120, axis=1), pltpu.roll(reduced, 112, axis=1)
    form = (c_real * first + c_imag * second) * gram_real - (c_real * second - c_imag * first) * gram_imag
    quadratic = jnp.sum(jnp.where(lane < KRYLOV, weight * form, 0.0)) * MEAN_SCALE
    linear = 2.0 * jnp.sum(jnp.where(lane < 2, dots * dots, 0.0))
    constant = jnp.sum(jnp.where(lane == 2, dots, 0.0))
    norm_square = constant - linear + quadratic
    fine = (norm_square > LEAST * (constant + linear + quadratic)) & (norm_square < MOST)
    norm_ref[0] = jnp.max(lax.rsqrt(jnp.full((8, 128), norm_square, F32)))
    flag_ref[0] = jnp.where(fine, 0, 1)

    for start, size in row_pieces(64, rows):
        place = pl.ds(start, size)
        plain = image[place, :]
        turned = jnp.zeros((size, 128), F32)
        for k in range(KRYLOV):
            vector = basis[pl.ds(k * rows + start, size), :]
            plain = plain - dots[k : k + 1, 0:1] * vector
            turned = turned + dots[k : k + 1, 1:2] * vector
        out_ref[place, :] = plain - times_i(turned)
    for copy in sends:
        copy.wait_send()


def shards(basis, mie_coeffs, rot_table, axial_table, pair_table, pair_count):
    rows = 2 * MODES
    anywhere = pl.BlockSpec(memory_space=pl.ANY)
    dots, vector, scale, flag = pl.pallas_call(
        kernel,
        out_shape=(
            jax.ShapeDtypeStruct((2, KRYLOV), F32),
            jax.ShapeDtypeStruct((rows, 2 * SPHERES), F32),
            jax.ShapeDtypeStruct((1,), F32),
            jax.ShapeDtypeStruct((1,), jnp.int32),
        ),
        in_specs=[anywhere] * 5 + [pl.BlockSpec(memory_space=pltpu.SMEM)],
        out_specs=(pl.BlockSpec(memory_space=pltpu.VMEM),) * 2 + (pl.BlockSpec(memory_space=pltpu.SMEM),) * 2,
        scratch_shapes=[
            pltpu.VMEM((KRYLOV * rows, 128), F32),
            pltpu.VMEM((MODES, 2, 128), F32),
            pltpu.VMEM((2, rows, 128), F32),
            pltpu.VMEM((MODES, TABLES, MODES), BF16),
            pltpu.VMEM((TABLES // 2, MODES, 2, MODES), BF16),
            pltpu.VMEM((TABLES, PAD, PAD), BF16),
            pltpu.VMEM((2, 2, PAD, PAD), BF16),
            pltpu.VMEM((TABLES, 2, PAD, PAD), BF16),
            pltpu.VMEM((3, 1, 128), jnp.int32),
            pltpu.VMEM((2, PAD, 128), F32),
            pltpu.VMEM((3, 8, 128), F32),
            pltpu.VMEM((12, 16, ROWS, PAD), BF16),
            pltpu.VMEM((8, 32, ROWS, PAD), BF16),
            pltpu.VMEM((2, 128, PAD), F32),
            pltpu.VMEM((2 * PAD, 128), F32),
            pltpu.VMEM((rows, 128), F32),
            pltpu.VMEM((1, 8, 8, 128), F32),
            pltpu.VMEM((1, 16, 8, 128), F32),
            pltpu.SemaphoreType.DMA((13,)),
            pltpu.SemaphoreType.DMA((11 * CHUNKS,)),
            pltpu.SemaphoreType.DMA((12 * CHUNKS,)),
            pltpu.SemaphoreType.DMA((2,)),
            pltpu.SemaphoreType.DMA((2,)),
            pltpu.SemaphoreType.DMA((1, 7)),
            pltpu.SemaphoreType.DMA((1, 8)),
            pltpu.SemaphoreType.DMA((1, 15)),
            pltpu.SemaphoreType.DMA((1, 16)),
            pltpu.SemaphoreType.DMA((TABLES // 2,)),
            pltpu.SemaphoreType.DMA((TABLES // 2,)),
            pltpu.SemaphoreType.REGULAR((4,)),
        ],
        compiler_params=pltpu.CompilerParams(
            collective_id=0, has_side_effects=True, vmem_limit_bytes=56 * 1024 * 1024
        ),
        name="arnoldi",
    )(
        jnp.transpose(basis, (0, 2, 1, 3)).reshape(KRYLOV * rows, 128),
        jnp.transpose(mie_coeffs, (1, 0, 2)),
        jnp.transpose(rot_table, (1, 0, 2)),
        jnp.transpose(axial_table, (0, 2, 1, 3)),
        jnp.transpose(pair_table, (2, 0, 1)),
        pair_count,
    )
    def direct(vector, scale):
        return lax.rsqrt(lax.psum(jnp.sum(vector * vector), ("blk", "pair")) * MEAN_SCALE)

    scale = lax.cond(flag[0] != 0, direct, lambda vector, scale: scale, vector, scale[0])
    vector = vector * scale
    return dots * MEAN_SCALE, jnp.transpose(vector.reshape(MODES, 2, 128), (1, 0, 2))


def solution(mesh):
    placed = (
        P(None, ("blk", "pair"), None, None),
        P(("blk", "pair"), None, None),
        P(),
        P(),
        P("blk", None, None),
        P("blk"),
    )
    return jax.shard_map(
        shards,
        mesh=mesh,
        in_specs=placed,
        out_specs=(P(), P(("blk", "pair"), None, None)),
        check_vma=False,
    )
```

```python
import functools

import jax
import jax.numpy as jnp
from jax import lax
from jax.experimental import pallas as pl
from jax.experimental.pallas import tpu as pltpu
from jax.sharding import PartitionSpec as P

MESH = pl.DeviceIdType.MESH
F32 = jnp.float32
BF16 = jnp.bfloat16
MODES = 510
PAD = 512
KRYLOV = 8
TABLES = 8
BLOCKS = 256
SPHERES = 64
ROWS = 16
CHUNKS = 2
LEAST = 0.01
MOST = 1e37
MEAN_SCALE = 1.0 / (BLOCKS * MODES * 2 * SPHERES)

NT = (((1,), (1,)), ((), ()))
NN = (((1,), (0,)), ((), ()))


def dot(left, right, dims):
    return lax.dot_general(left, right, dims, preferred_element_type=F32)


def times_i(value):
    lane = lax.broadcasted_iota(jnp.int32, value.shape, 1)
    turned = pltpu.roll(value, SPHERES, axis=1)
    return jnp.where(lane < SPHERES, -turned, turned)


def fold(value):
    rows = value.shape[0]
    whole = rows // 8 * 8
    total = value[:8]
    for start in range(8, whole, 8):
        total = total + value[start : start + 8]
    if rows > whole:
        rest = value[whole:]
        total = total + jnp.concatenate([rest, jnp.zeros((8 - rest.shape[0], 128), F32)], axis=0)
    return total


def row_pieces(step, total):
    return [(start, min(step, total - start)) for start in range(0, total, step)]


def count_matrix(pairs, member):
    row = lax.broadcasted_iota(jnp.int32, (256, 128), 0)
    g_row = (row >> 5).astype(F32)
    back = ((row >> 4) & 1) == 1
    own = (2 * member + ((row >> 3) & 1)).astype(F32)
    column = (lax.broadcasted_iota(jnp.int32, (192, 128), 0) >> 3).astype(F32)
    total = None
    for off, back_here in ((1, False), (0, True), (1, True), (2, True)):
        a, b, g = (pairs[off, n : n + 1, :] for n in range(3))
        right_table = jnp.where(g_row == g, 1.0, 0.0)
        if back_here:
            hit = jnp.where(back & (own + 8.0 * (2 - off) == b), right_table, 0.0)
            place = jnp.where(column == a + 8.0 * off, 1.0, 0.0)
        else:
            hit = jnp.where((~back) & (own == a), right_table, 0.0)
            place = jnp.where(column == b, 1.0, 0.0)
        term = dot(hit.astype(BF16), place.astype(BF16), NT)
        total = term if total is None else total + term
    same = (lax.broadcasted_iota(jnp.int32, (256, 192), 0) & 7) == (
        lax.broadcasted_iota(jnp.int32, (256, 192), 1) & 7
    )
    return jnp.where(same, total, 0.0).astype(BF16)


def aggregate(counts, win, sums, group):
    halves = []
    for slab in (2 * group, 2 * group + 1):
        part = win[:, slab].reshape(12 * ROWS, PAD)
        halves.append(dot(counts, part, NN).reshape(32, 8, PAD))
    sums[group] = jnp.concatenate(halves, axis=1).astype(BF16)


def field_of(sums, operators, field):
    groups = [[half * 4 + imag * 2 + n for half in range(2) for n in range(2)] for imag in range(2)]

    def gathered(g, direction):
        parts = []
        for imag in range(2):
            for t in range(2):
                parts.extend(sums[n, g * 4 + direction * 2 + t] for n in groups[imag])
        value = jnp.concatenate(parts, axis=0)
        return value, jnp.concatenate([-value[128:], value[:128]], axis=0)

    total = None
    for g in range(TABLES):
        for direction, dims in ((0, NT), (1, NN)):
            for part, value in enumerate(gathered(g, direction)):
                term = dot(value, operators[g, part], dims)
                total = term if total is None else total + term
    for imag in range(2):
        for t in range(2):
            start = (imag * 2 + t) * 64
            field[t, imag * 64 : imag * 64 + 64] = total[start : start + 64]


def kernel(
    basis_hbm, mie_hbm, rot_hbm, axial_hbm, table_hbm, count_ref,
    proj_ref, out_ref, norm_ref, flag_ref,
    basis, mie_raw, mie, rot_raw, axial_raw, rot, axial, operators, table, current, pairs, win, sums, field, mixed, image, red_a, red_b,
    load_sem, send_sem, recv_sem, pair_send, pair_recv, a_send, a_recv, b_send, b_recv, share_send, share_recv, far_sem,
):
    blk_ways, pair_ways = lax.axis_size("blk"), lax.axis_size("pair")
    blk, member = lax.axis_index("blk"), lax.axis_index("pair")
    core = lax.rem(blk, 2)
    row = blk // 2
    row_ways = blk_ways // 2
    inner = blk + 1 - 2 * core
    outer = lax.rem(blk - 1 + 2 * core + blk_ways, blk_ways)
    right, left, far = (lax.rem(member + n, pair_ways) for n in (1, 3, 2))

    last = KRYLOV - 1
    rows = 2 * MODES
    share = TABLES // 2
    first_rows = last * rows // 8 * 8
    head, tail = pl.ds(0, first_rows), pl.ds(first_rows, KRYLOV * rows - first_rows)
    load_last = pltpu.make_async_copy(basis_hbm.at[tail], basis.at[tail], load_sem.at[0])
    load_table = pltpu.make_async_copy(table_hbm, table, load_sem.at[1])
    load_rot = pltpu.make_async_copy(rot_hbm, rot_raw, load_sem.at[2])
    load_axial = [
        pltpu.make_async_copy(axial_hbm.at[core * share + n], axial_raw.at[n], load_sem.at[5 + n])
        for n in range(share)
    ]
    load_rest = pltpu.make_async_copy(basis_hbm.at[head], basis.at[head], load_sem.at[3])
    load_mie = pltpu.make_async_copy(mie_hbm, mie_raw, load_sem.at[4])
    for load in [load_last, load_table, load_rot, *load_axial, load_rest, load_mie]:
        load.start()

    spot = core * pair_ways + member
    group_a = []
    for n in (2, 6, 1, 3, 5, 7, 4):
        other = lax.rem(spot + n, 2 * pair_ways)
        group_a.append((other, (2 * row + other // pair_ways, lax.rem(other, pair_ways))))
    group_b = []
    high, low = row // 4, lax.rem(row, 4)
    steps = [(n, m) for n in range(4) for m in range(4) if n or m]
    for n, m in sorted(steps, key=lambda step: -min(step[0], 4 - step[0]) - min(step[1], 4 - step[1])):
        other = 4 * lax.rem(high + n, 4) + lax.rem(low + m, 4)
        group_b.append((other, (2 * other + core, member)))
    barrier = pltpu.get_barrier_semaphore()
    def beside(distance):
        steps = (distance, row_ways - distance)
        return [(2 * lax.rem(row + n, row_ways) + core, member) for n in steps]

    near = [(outer, member), (blk, right), (blk, left), (inner, member)]
    rounds = [near, [(inner, member)] + beside(1), beside(2), beside(4)]
    for device in near:
        pl.semaphore_signal(barrier, inc=1, device_id=device, device_id_type=MESH)

    def pass_on(turn):
        if turn:
            pl.semaphore_wait(far_sem.at[turn - 1], len(rounds[turn - 1]))
        for device in rounds[turn]:
            pl.semaphore_signal(far_sem.at[turn], inc=1, device_id=device, device_id_type=MESH)

    load_last.wait()
    current[:, pl.ds(MODES - 6, 8), :] = jnp.zeros((2, 8, 128), F32)
    mine = 4 + member
    for t in range(2):
        current[t, pl.ds(0, MODES), :] = basis[pl.ds(last * rows + t, MODES, stride=2), :]
    flipped = [jnp.transpose(current[t]) for t in range(2)]

    def place(half):
        for slab in range(8 * half, 8 * half + 8):
            start = slab // 4 % 2 * 64 + half * 32 + slab % 4 * 8
            both = jnp.concatenate([value[start : start + 8] for value in flipped], axis=0)
            win[mine, slab] = both.astype(BF16)

    place(0)
    place(1)
    pl.semaphore_wait(barrier, len(near))

    width = 16 // CHUNKS
    sends = []
    window_sends = list(range(11 * CHUNKS))

    def send(source_slot, target_slot, chunk, device):
        span = pl.ds(chunk * width, width)
        copy = pltpu.make_async_remote_copy(
            src_ref=win.at[source_slot, span],
            dst_ref=win.at[target_slot, span],
            send_sem=send_sem.at[window_sends.pop()],
            recv_sem=recv_sem.at[target_slot * CHUNKS + chunk],
            device_id=device,
            device_id_type=MESH,
        )
        copy.start()
        sends.append(copy)

    def arrived(slot, chunk):
        span = pl.ds(chunk * width, width)
        pltpu.make_async_remote_copy(
            src_ref=win.at[slot, span],
            dst_ref=win.at[slot, span],
            send_sem=send_sem.at[0],
            recv_sem=recv_sem.at[slot * CHUNKS + chunk],
            device_id=(inner, member),
            device_id_type=MESH,
        ).wait_recv()

    to_inner, to_outer = 8 * core, 8 * (1 - core)
    from_inner, from_outer = 8 * (1 - core), 8 * core
    for chunk in range(CHUNKS):
        send(mine, to_outer + member, chunk, (outer, member))
        send(mine, mine, chunk, (blk, right))
        send(mine, mine, chunk, (blk, left))
        send(mine, to_inner + member, chunk, (inner, member))

    load_table.wait()
    live = lax.broadcasted_iota(jnp.int32, (1, 128), 1) < count_ref[0]
    pairs[1, pl.ds(0, 1), :] = table[0].astype(F32)
    pairs[1, pl.ds(1, 1), :] = table[1].astype(F32)
    pairs[1, pl.ds(2, 1), :] = jnp.where(live, table[2].astype(F32), -1.0)
    pairs[1, pl.ds(3, 5), :] = jnp.zeros((5, 128), F32)
    pair_copies = []
    for n, (slot, device) in enumerate(((2 * core, (inner, member)), (2 - 2 * core, (outer, member)))):
        copy = pltpu.make_async_remote_copy(
            src_ref=pairs.at[1],
            dst_ref=pairs.at[slot],
            send_sem=pair_send.at[n],
            recv_sem=pair_recv.at[n],
            device_id=device,
            device_id_type=MESH,
        )
        copy.start()
        pair_copies.append(copy)

    def forward(chunk):
        for origin, keep_on, device in ((left, 0, right), (right, 1, left)):
            arrived(4 + origin, chunk)
            if chunk % 2 == keep_on:
                send(4 + origin, 4 + origin, chunk, (blk, device))
            send(4 + origin, to_outer + origin, chunk, (outer, member))
            send(4 + origin, to_inner + origin, chunk, (inner, member))

    def forward_far(chunk):
        arrived(4 + far, chunk)
        send(4 + far, to_outer + far, chunk, (outer, member))
        send(4 + far, to_inner + far, chunk, (inner, member))

    def landed(chunks):
        for chunk in chunks:
            for n in range(pair_ways):
                arrived(from_inner + n, chunk)
                arrived(from_outer + n, chunk)

    rot[:, pl.ds(PAD - 16, 16), :] = jnp.zeros((TABLES, 16, PAD), BF16)
    rot[:, :, pl.ds(PAD - 128, 128)] = jnp.zeros((TABLES, PAD, 128), BF16)

    def order_rot():
        load_rot.wait()
        for start, size in row_pieces(32, MODES):
            value = rot_raw[pl.ds(start, size)]
            rot[:, pl.ds(start, size), pl.ds(0, MODES)] = jnp.swapaxes(value, 0, 1)

    def order_axial(g):
        for start, size in row_pieces(64, MODES):
            value = axial_raw[g, pl.ds(start, size)]
            axial[g % 2, :, pl.ds(start, size), pl.ds(0, MODES)] = jnp.swapaxes(value, 0, 1)

    def shared(n, first):
        place = operators.at[first + n]
        return pltpu.make_async_remote_copy(
            src_ref=place,
            dst_ref=place,
            send_sem=share_send.at[n],
            recv_sem=share_recv.at[n],
            device_id=(inner, member),
            device_id_type=MESH,
        )

    def operator(n):
        g = core * share + n
        rotation = rot[g]
        flipped = jnp.transpose(rotation)
        for part in range(2):
            moved = dot(axial[n % 2, part], rotation, NN).astype(BF16)
            operators[g, part] = dot(flipped, moved, NN).astype(BF16)
        copy = shared(n, core * share)
        copy.start()
        sends.append(copy)

    lines = []

    def gram_line(j):
        lane = lax.broadcasted_iota(jnp.int32, (1, 128), 1)
        real = [jnp.zeros((8, 128), F32)] * KRYLOV
        imag = [jnp.zeros((8, 128), F32)] * KRYLOV
        for start, size in row_pieces(64, rows):
            one = basis[pl.ds(j * rows + start, size), :]
            turned = times_i(one)
            for k in range(j, KRYLOV):
                other = basis[pl.ds(k * rows + start, size), :]
                real[k] = real[k] + fold(one * other)
                if k > j:
                    imag[k] = imag[k] + fold(turned * other)
        line = jnp.zeros((1, 128), F32)
        for k in range(j, KRYLOV):
            line = jnp.where(lane == 8 + k, jnp.sum(real[k]), line)
            if k > j:
                line = jnp.where(lane == 16 + k, jnp.sum(imag[k]), line)
        lines.append(line)

    def order_mie():
        for start, size in row_pieces(32, MODES):
            scale = mie_raw[pl.ds(start, size)].reshape(2 * size, 128)
            lane = lax.broadcasted_iota(jnp.int32, scale.shape, 1)
            other = pltpu.roll(scale, SPHERES, axis=1)
            mie[0, pl.ds(2 * start, 2 * size), :] = jnp.where(lane < SPHERES, scale, other)
            mie[1, pl.ds(2 * start, 2 * size), :] = jnp.where(lane < SPHERES, other, scale)

    axial[:, :, pl.ds(PAD - 16, 16), :] = jnp.zeros((2, 2, 16, PAD), BF16)
    axial[:, :, :, pl.ds(PAD - 128, 128)] = jnp.zeros((2, 2, PAD, 128), BF16)
    pass_on(0)
    order_rot()
    load_axial[0].wait()
    order_axial(0)
    load_axial[1].wait()
    order_axial(1)
    operator(0)
    load_axial[2].wait()
    order_axial(2)
    operator(1)
    forward(0)
    load_axial[3].wait()
    load_rest.wait()
    order_axial(3)
    operator(2)
    gram_line(0)
    pass_on(1)
    forward(1)
    operator(3)
    pass_on(2)
    forward_far(0)
    forward_far(1)
    pass_on(3)
    gram_line(1)
    gram_line(2)
    load_mie.wait()
    for copy in pair_copies:
        copy.wait()
    for j in range(3, KRYLOV):
        gram_line(j)
    packed_gram = jnp.concatenate(lines, axis=0)
    counts = count_matrix(pairs, member)
    order_mie()
    pl.semaphore_wait(far_sem.at[3], len(rounds[3]))
    for n in range(share):
        shared(n, (1 - core) * share).wait_recv()
    landed(range(CHUNKS))
    for group in range(8):
        aggregate(counts, win, sums, group)
    field_of(sums, operators, field)

    real = [jnp.zeros((8, 128), F32)] * KRYLOV
    imag = [jnp.zeros((8, 128), F32)] * KRYLOV
    square = jnp.zeros((8, 128), F32)
    for t in range(2):
        mixed[pl.ds(t, PAD, stride=2), :] = jnp.transpose(field[t])
    for start, size in row_pieces(64, rows):
        place = pl.ds(start, size)
        here = mixed[place, :]
        product = mie[0, place, :] * here + mie[1, place, :] * times_i(here)
        value = basis[pl.ds(last * rows + start, size), :] - product
        image[place, :] = value
        turned = times_i(value)
        square = square + fold(value * value)
        for k in range(KRYLOV):
            vector = basis[pl.ds(k * rows + start, size), :]
            real[k] = real[k] + fold(vector * value)
            imag[k] = imag[k] - fold(vector * turned)

    def tile_of(parts):
        rows = [jnp.sum(part, axis=0, keepdims=True) for part in parts]
        return jnp.sum(jnp.concatenate(rows, axis=0), axis=1, keepdims=True)

    def all_sum(call, value):
        steps = ((red_a, a_send, a_recv, group_a, spot), (red_b, b_send, b_recv, group_b, row))
        for store, send_sems, recv_sems, group, index in steps:
            store[call, index] = value
            copies = []
            for n, (other, device) in enumerate(group):
                copy = pltpu.make_async_remote_copy(
                    src_ref=store.at[call, index],
                    dst_ref=store.at[call, index],
                    send_sem=send_sems.at[call, n],
                    recv_sem=recv_sems.at[call, index],
                    device_id=device,
                    device_id_type=MESH,
                )
                copy.start()
                copies.append(copy)
            for copy in sends:
                copy.wait_send()
            sends.clear()
            for other, device in group:
                pltpu.make_async_remote_copy(
                    src_ref=store.at[call, other],
                    dst_ref=store.at[call, other],
                    send_sem=send_sems.at[call, 0],
                    recv_sem=recv_sems.at[call, other],
                    device_id=device,
                    device_id_type=MESH,
                ).wait_recv()
            value = store[call, 0]
            for n in range(1, len(group) + 1):
                value = value + store[call, n]
            sends.extend(copies)
        return value

    lane = lax.broadcasted_iota(jnp.int32, (8, 128), 1)
    packed = jnp.where(lane == 0, tile_of(real), jnp.where(lane == 1, tile_of(imag), packed_gram))
    packed = jnp.where(lane == 2, jnp.sum(square) * 0.125, packed)
    reduced = all_sum(0, packed)
    dots = reduced * MEAN_SCALE
    turned_dots = jnp.transpose(jnp.concatenate([dots, jnp.zeros((120, 128), F32)], axis=0))
    proj_ref[...] = jnp.transpose(jnp.concatenate([reduced, jnp.zeros((120, 128), F32)], axis=0))[:2, :KRYLOV]

    first, second = jnp.where(lane < KRYLOV, turned_dots[0:1], 0.0), jnp.where(lane < KRYLOV, turned_dots[1:2], 0.0)
    c_real, c_imag = dots[:, 0:1], dots[:, 1:2]
    weight = jnp.where(lane == lax.broadcasted_iota(jnp.int32, (8, 128), 0), 1.0, 2.0)
    gram_real, gram_imag = pltpu.roll(reduced, 120, axis=1), pltpu.roll(reduced, 112, axis=1)
    form = (c_real * first + c_imag * second) * gram_real - (c_real * second - c_imag * first) * gram_imag
    quadratic = jnp.sum(jnp.where(lane < KRYLOV, weight * form, 0.0)) * MEAN_SCALE
    linear = 2.0 * jnp.sum(jnp.where(lane < 2, dots * dots, 0.0))
    constant = jnp.sum(jnp.where(lane == 2, dots, 0.0))
    norm_square = constant - linear + quadratic
    fine = (norm_square > LEAST * (constant + linear + quadratic)) & (norm_square < MOST)
    norm_ref[0] = jnp.max(lax.rsqrt(jnp.full((8, 128), norm_square, F32)))
    flag_ref[0] = jnp.where(fine, 0, 1)

    for start, size in row_pieces(64, rows):
        place = pl.ds(start, size)
        plain = image[place, :]
        turned = jnp.zeros((size, 128), F32)
        for k in range(KRYLOV):
            vector = basis[pl.ds(k * rows + start, size), :]
            plain = plain - dots[k : k + 1, 0:1] * vector
            turned = turned + dots[k : k + 1, 1:2] * vector
        out_ref[place, :] = plain - times_i(turned)
    for copy in sends:
        copy.wait_send()


def shards(basis, mie_coeffs, rot_table, axial_table, pair_table, pair_count):
    rows = 2 * MODES
    anywhere = pl.BlockSpec(memory_space=pl.ANY)
    dots, vector, scale, flag = pl.pallas_call(
        kernel,
        out_shape=(
            jax.ShapeDtypeStruct((2, KRYLOV), F32),
            jax.ShapeDtypeStruct((rows, 2 * SPHERES), F32),
            jax.ShapeDtypeStruct((1,), F32),
            jax.ShapeDtypeStruct((1,), jnp.int32),
        ),
        in_specs=[anywhere] * 5 + [pl.BlockSpec(memory_space=pltpu.SMEM)],
        out_specs=(pl.BlockSpec(memory_space=pltpu.VMEM),) * 2 + (pl.BlockSpec(memory_space=pltpu.SMEM),) * 2,
        scratch_shapes=[
            pltpu.VMEM((KRYLOV * rows, 128), F32),
            pltpu.VMEM((MODES, 2, 128), F32),
            pltpu.VMEM((2, rows, 128), F32),
            pltpu.VMEM((MODES, TABLES, MODES), BF16),
            pltpu.VMEM((TABLES // 2, MODES, 2, MODES), BF16),
            pltpu.VMEM((TABLES, PAD, PAD), BF16),
            pltpu.VMEM((2, 2, PAD, PAD), BF16),
            pltpu.VMEM((TABLES, 2, PAD, PAD), BF16),
            pltpu.VMEM((3, 1, 128), jnp.int32),
            pltpu.VMEM((2, PAD, 128), F32),
            pltpu.VMEM((3, 8, 128), F32),
            pltpu.VMEM((12, 16, ROWS, PAD), BF16),
            pltpu.VMEM((8, 32, ROWS, PAD), BF16),
            pltpu.VMEM((2, 128, PAD), F32),
            pltpu.VMEM((2 * PAD, 128), F32),
            pltpu.VMEM((rows, 128), F32),
            pltpu.VMEM((1, 8, 8, 128), F32),
            pltpu.VMEM((1, 16, 8, 128), F32),
            pltpu.SemaphoreType.DMA((13,)),
            pltpu.SemaphoreType.DMA((11 * CHUNKS,)),
            pltpu.SemaphoreType.DMA((12 * CHUNKS,)),
            pltpu.SemaphoreType.DMA((2,)),
            pltpu.SemaphoreType.DMA((2,)),
            pltpu.SemaphoreType.DMA((1, 7)),
            pltpu.SemaphoreType.DMA((1, 8)),
            pltpu.SemaphoreType.DMA((1, 15)),
            pltpu.SemaphoreType.DMA((1, 16)),
            pltpu.SemaphoreType.DMA((TABLES // 2,)),
            pltpu.SemaphoreType.DMA((TABLES // 2,)),
            pltpu.SemaphoreType.REGULAR((4,)),
        ],
        compiler_params=pltpu.CompilerParams(
            collective_id=0, has_side_effects=True, vmem_limit_bytes=56 * 1024 * 1024
        ),
        name="arnoldi",
    )(
        jnp.transpose(basis, (0, 2, 1, 3)).reshape(KRYLOV * rows, 128),
        jnp.transpose(mie_coeffs, (1, 0, 2)),
        jnp.transpose(rot_table, (1, 0, 2)),
        jnp.transpose(axial_table, (0, 2, 1, 3)),
        jnp.transpose(pair_table, (2, 0, 1)),
        pair_count,
    )
    def direct(vector, scale):
        return lax.rsqrt(lax.psum(jnp.sum(vector * vector), ("blk", "pair")) * MEAN_SCALE)

    scale = lax.cond(flag[0] != 0, direct, lambda vector, scale: scale, vector, scale[0])
    vector = vector * scale
    return dots * MEAN_SCALE, jnp.transpose(vector.reshape(MODES, 2, 128), (1, 0, 2))


def solution(mesh):
    placed = (
        P(None, ("blk", "pair"), None, None),
        P(("blk", "pair"), None, None),
        P(),
        P(),
        P("blk", None, None),
        P("blk"),
    )
    return jax.shard_map(
        shards,
        mesh=mesh,
        in_specs=placed,
        out_specs=(P(), P(("blk", "pair"), None, None)),
        check_vma=False,
    )
```
